256 devices in a mesh: space: 32 (over x, y, core), chan: 8 (over z).
Axes of the slice: x: 4, y: 4, z: 8, core: 2. Of those that a mesh axis runs over, the one named last changes fastest.
Arguments:
- features: bfloat16 [64, 16, 16, 1024], P('space', None, None, 'chan'), may hold values from -6 to 6
- filters: bfloat16 [1024, 27, 1024], P('space', None, 'chan'), may hold values from -0.0390625 to 0.0390625
- conv_bias: float32 [1024], P('chan'), may hold values from -3 to 3
- cotangent: bfloat16 [64, 16, 16, 1024], P('space', None, None, 'chan'), may hold values from -6 to 6
Outputs:
- activated: bfloat16 [64, 16, 16, 1024], P('space', None, None, 'chan')
- grad_input: bfloat16 [64, 16, 16, 1024], P('space', None, None, 'chan')
- grad_filters: float32 [1024, 27, 1024], P('space', None, 'chan')
- grad_bias: float32 [1024], P('chan')
The draws below stay inside these ranges and needn't reach their ends.
All inputs are finite; a program needn't handle non-finite values.
Results may differ from the reference program's by a relative error of at most 0.007.
Values may be sent and summed in bfloat16 or wider, within the bound.
No kernel may reach another device: no remote copies, remote signals or barrier semaphores. Data moves between devices by JAX's collectives and lax.ppermute only.
A program may use at most 128 MiB of HBM per device.

```python
import math
import jax
import jax.numpy as jnp
from jax import lax

GRID = 16
CIN = 1024
COUT = 1024
PLANES = 64
CELLS = 16384


def raised(drawn, own_key, source, target, blocks, factor):
    owner, partner = [(jnp.arange(drawn.shape[position]) // (drawn.shape[position] // blocks)).reshape([-1 if axis == position else 1 for axis in range(drawn.ndim)]) for position in (source, target)]
    chosen = jax.random.permutation(own_key, blocks)[partner]
    strong = (owner == chosen) | (owner == (partner + blocks // 2) % blocks)
    return jnp.where(strong, factor * drawn, drawn)


def block_levels(key, extent, pieces, low, top_value):
    level, own = 1.0, jax.random.fold_in(key, 6)
    for position, blocks in pieces:
        draws = jnp.exp(jax.random.uniform(jax.random.fold_in(own, position), (blocks,), jnp.float32, low / len(pieces), top_value / len(pieces)))
        level = level * jnp.repeat(draws, extent[position] // blocks).reshape([-1 if axis == position else 1 for axis in range(len(extent))])
    return level


def bell_draw(rng, dims, deviation, limit, cuts=(), kind=jnp.bfloat16):
    drawn = jax.random.normal(rng, dims, jnp.float32) * deviation
    if len(cuts) > 0:
        drawn = block_levels(rng, dims, cuts, -0.22, 0.18) * drawn
    return jnp.clip(drawn, min=-limit, max=limit).astype(kind)


def noise_with(rng, dims, scale, reach, split, heavy, kind=jnp.bfloat16):
    array = scale * jax.random.normal(rng, dims, jnp.float32)
    if split:
        array = array * block_levels(rng, dims, split, -0.22, 0.18)
    return jnp.clip(raised(array, jax.random.fold_in(rng, 3), *heavy), -reach, reach).astype(kind)


def setup_inputs(seed: int = 0) -> dict:
    splits = jax.random.split(jax.random.key(seed), 5)
    return {
        "features": noise_with(splits[0], (PLANES, GRID, GRID, CIN), 1.0, 6.0, ((0, 32), (3, 8)), (0, 3, 32, 2.75)),
        "filters": bell_draw(splits[1], (CIN, 27, COUT), (27 * CIN) ** -0.5, 0.0390625, ((0, 32), (2, 8))),
        "conv_bias": bell_draw(splits[2], (COUT,), 0.5, 3.0, ((0, 8),), jnp.float32),
        "cotangent": bell_draw(splits[3], (PLANES, GRID, GRID, COUT), 1.0, 6.0, ((0, 32), (3, 8))),
    }


KAPPA = 0.7978845608028654
CUBIC = 0.044715

def gelu_pair(values):
    inner = KAPPA * (values + CUBIC * values * values * values)
    tangent = jnp.tanh(inner)
    output = 0.5 * values * (1.0 + tangent)
    slope = 0.5 * (1.0 + tangent) + 0.5 * values * (1.0 - tangent * tangent) * KAPPA * (1.0 + 3.0 * CUBIC * values * values)
    return (output, slope)

def padded_samples(planes_in):
    channels = planes_in.shape[-1]
    samples = planes_in.reshape(-1, GRID, GRID, GRID, channels)
    return jnp.pad(samples, ((0, 0), (1, 1), (1, 1), (1, 1), (0, 0)))

def tap_window(padded, tap_index):
    depth_off = tap_index // 9
    height_off = tap_index // 3 % 3
    width_off = tap_index % 3
    window_cells = padded[:, depth_off:depth_off + GRID, height_off:height_off + GRID, width_off:width_off + GRID, :]
    return window_cells.reshape(-1, padded.shape[-1])

def reference(features, filters, conv_bias, cotangent):
    rolled_features = jnp.roll(features, -1, axis=0)
    rolled_cotangent = jnp.roll(cotangent, -1, axis=0)
    feature_pad = padded_samples(rolled_features)
    summed = jnp.zeros((CELLS, COUT), jnp.float32)
    for tap_index in range(27):
        summed = summed + jnp.dot(tap_window(feature_pad, tap_index), filters[:, tap_index, :], preferred_element_type=jnp.float32)
    pre_act = summed + conv_bias.astype(jnp.float32)[None, :]
    output, slope = gelu_pair(pre_act)
    activated = jnp.roll(output.astype(jnp.bfloat16).reshape(PLANES, GRID, GRID, COUT), 1, axis=0)
    grad_pre = (rolled_cotangent.astype(jnp.float32).reshape(CELLS, COUT) * slope).astype(jnp.bfloat16)
    scale = 1.0 / math.sqrt(CELLS)
    grad_bias = lax.optimization_barrier(jnp.sum(grad_pre.astype(jnp.float32), axis=0)) * scale
    grad_pad = padded_samples(grad_pre.reshape(PLANES, GRID, GRID, COUT))
    backward = jnp.zeros((CELLS, CIN), jnp.float32)
    for tap_index in range(27):
        backward = backward + jnp.dot(tap_window(grad_pad, 26 - tap_index), filters[:, tap_index, :].T, preferred_element_type=jnp.float32)
    grad_input = jnp.roll(backward.astype(jnp.bfloat16).reshape(PLANES, GRID, GRID, CIN), 1, axis=0)
    terms = []
    for tap_index in range(27):
        product = lax.dot_general(tap_window(feature_pad, tap_index), grad_pre, (((0,), (0,)), ((), ())), preferred_element_type=jnp.float32)
        terms.append(product * scale)
    grad_filters = jnp.stack(terms, axis=1)
    return (activated, grad_input, grad_filters, grad_bias)
```

```python
import math

import jax
import jax.numpy as jnp
from jax import lax
from jax.experimental import pallas as pl
from jax.experimental.pallas import tpu as pltpu
from jax.sharding import PartitionSpec as P


GRID = 16
FACE = GRID * GRID
NX, NQ, NZ = 4, 8, 8
KAPPA = 0.7978845608028654
CUBIC = 0.044715
VMEM_LIMIT = 24 * 1024 * 1024
Z_STEPS = (0, 1, -1, 4, 2, -3, -2, 3)


def gelu_pair(values):
    inner = KAPPA * (values + CUBIC * values * values * values)
    tangent = jnp.tanh(inner)
    output = 0.5 * values * (1.0 + tangent)
    slope = 0.5 * (1.0 + tangent) + 0.5 * values * (1.0 - tangent * tangent) * KAPPA * (
        1.0 + 3.0 * CUBIC * values * values
    )
    return (output, slope)


def device(space, z):
    return space % (NX * NQ) * NZ + z % NZ


def at(x, q, z):
    return device(x % NX * NQ + q % NQ, z)


def permuted(array, target):
    pairs = [(at(x, q, z), target(x, q, z)) for x in range(NX) for q in range(NQ) for z in range(NZ)]
    return lax.ppermute(array, ("space", "chan"), pairs)


def group(q):
    return q // 2 + 4 * (q % 2)


def holder(group):
    return group % 4 * 2 + group // 4


def swapped(index):
    return index >> 1 | (index & 1) << 1


def position(where):
    space, z = where[0], where[1]
    q = space & (NQ - 1)
    return space >> 3, q, q >> 1, q & 1, z


def ring_pairs(where, steps):
    _, _, y, core, z = position(where)
    return [(z + r - y - 4 * core) & (NQ - 1) for r in steps]


def slope_pairs(where):
    _, _, y, core, _ = position(where)
    rows = [(y - r) & 3 for r in range(4)]
    return [2 * row + core for row in rows] + [2 * row + 1 - core for row in rows]


def store_columns(pairs, planes, columns):
    size = planes[0].shape[-1]
    width = lax.broadcasted_iota(jnp.int32, (FACE, size), 0) % GRID
    rows, whole = columns.shape[1:]
    columns[0] = jnp.zeros((rows, whole), jnp.bfloat16)
    columns[GRID + 1] = jnp.zeros((rows, whole), jnp.bfloat16)
    edge = jnp.zeros((GRID, whole), jnp.bfloat16)
    places = [(ref, 2 * index) for ref in planes for index in range(ref.shape[0] // 2)]
    for pair, (ref, start) in zip(pairs, places):
        for half in range(2):
            depth = 2 * pair + half + 1
            middle = ref[start + half]
            wide = middle.astype(jnp.float32)
            left = jnp.where(width == 0, 0.0, pltpu.roll(wide, 1, 0)).astype(jnp.bfloat16)
            right = jnp.where(width == GRID - 1, 0.0, pltpu.roll(wide, FACE - 1, 0)).astype(
                jnp.bfloat16
            )
            columns[depth, :GRID, :] = edge
            columns[depth, FACE + GRID :, :] = edge
            for c, value in enumerate((left, middle, right)):
                columns[depth, GRID : FACE + GRID, c * size : (c + 1) * size] = value


def window(columns, plane):
    return jnp.concatenate(
        [columns[plane, GRID * b : GRID * b + FACE, :] for b in range(3)], axis=1
    )


def convolved(columns, pairs, paired):
    product = None
    for j in range(2):
        left = jnp.concatenate(
            [
                jnp.concatenate([window(columns, 2 * pair + 2 * j + i) for i in range(2)], axis=1)
                for pair in pairs
            ],
            axis=0,
        )
        part = jnp.dot(left, paired[j], preferred_element_type=jnp.float32)
        product = part if product is None else product + part
    return product


def halves(product, index, size):
    rows = slice(index * FACE, (index + 1) * FACE)
    return [product[rows, o * size : (o + 1) * size] for o in range(2)]


def weights_kernel(where, *refs):
    blocks = refs[:NX]
    ahead, back, natural = refs[NX:]
    size, out_size, rows = natural.shape[1], natural.shape[2], blocks[0].shape[1]
    x = position(where)[0]
    for r in range(NX):
        offset = pl.multiple_of(swapped((x + r) & (NX - 1)) * rows, rows)
        for tap in range(27):
            natural[tap, pl.ds(offset, rows)] = blocks[r][tap]

    def store(ref, a, bc, block):
        height, width = block.shape
        for o in range(2):
            i = a + o
            first = ((i % 2) * 9 + bc) * height
            ref[i // 2, first : first + height, o * width : (o + 1) * width] = block

    for ref, height, width in ((ahead, size, out_size), (back, out_size, size)):
        none = jnp.zeros((9 * height, width), jnp.bfloat16)
        ref[0, : 9 * height, width:] = none
        ref[1, 9 * height :, :width] = none
    for tap in range(27):
        block = natural[tap]
        store(ahead, tap // 9, tap % 9, block)
        turned = block.astype(jnp.float32).T.astype(jnp.bfloat16)
        store(back, (26 - tap) // 9, (26 - tap) % 9, turned)


def forward_kernel(where, *refs):
    *planes, paired, keep, send, columns, total = refs
    size = total.shape[-1]
    _, _, y, core, _ = position(where)
    store_columns(ring_pairs(where, Z_STEPS), planes, columns)

    def step(index, carry):
        product = convolved(columns, [4 * index + p for p in range(4)], paired)
        for p in range(4):
            for o, value in enumerate(halves(product, p, size)):
                total[4 * index + p, o] = value
        return carry

    lax.fori_loop(0, NQ // 4, step, 0)
    for r in range(4):
        row = (y + r) & 3
        for half in range(2):
            keep[r, half] = total[2 * row + core, half]
            send[r, half] = total[2 * row + 1 - core, half].astype(jnp.bfloat16)


def slopes_kernel(where, *refs):
    store_columns(slope_pairs(where), refs[:NQ], refs[NQ])


def backward_kernel(steps, where, columns, paired, *outs):
    product = convolved(columns, ring_pairs(where, steps), paired)
    places = [(out, 2 * index) for out in outs for index in range(out.shape[0] // 2)]
    for index, (out, start) in enumerate(places):
        for half, value in enumerate(halves(product, index, out.shape[-1])):
            out[start + half] = value.astype(out.dtype)


def filters_kernel(scale, where, columns, *refs):
    planes, outs = refs[:NQ], refs[NQ : NQ + NX]
    turned, total, natural = refs[NQ + NX :]
    size, rows = natural.shape[-1], outs[0].shape[1]
    x = position(where)[0]
    turned[:, :FACE] = jnp.zeros((size, FACE), jnp.bfloat16)
    turned[:, (GRID + 1) * FACE :] = jnp.zeros((size, FACE), jnp.bfloat16)
    bias = jnp.zeros((8, size), jnp.float32)
    for pair, ref in zip(slope_pairs(where), planes):
        for half in range(2):
            value = ref[half].astype(jnp.float32)
            bias = bias + jnp.sum(value.reshape(FACE // 8, 8, size), axis=0)
            start = pl.multiple_of((2 * pair + half + 1) * FACE, FACE)
            turned[:, pl.ds(start, FACE)] = value.T.astype(jnp.bfloat16)
    total[...] = jnp.zeros_like(total)

    def step(index, carry):
        first = 8 * index
        left = jnp.concatenate(
            [
                turned[:, pl.ds(pl.multiple_of((first + 2 - a) * FACE, FACE), 8 * FACE)]
                for a in range(3)
            ],
            axis=0,
        )
        right = jnp.concatenate([window(columns, first + 1 + e) for e in range(8)], axis=0)
        total[...] += jnp.dot(left, right, preferred_element_type=jnp.float32)
        return carry

    lax.fori_loop(0, GRID // 8, step, 0)
    for tap in range(27):
        a, bc = tap // 9, tap % 9
        block = total[a * size : (a + 1) * size, bc * size : (bc + 1) * size]
        natural[tap] = block.T * scale
    whole = jnp.sum(bias, axis=0, keepdims=True) * scale
    upper = whole.astype(jnp.bfloat16)
    lower = (whole - upper.astype(jnp.float32)).astype(jnp.bfloat16)
    row = lax.broadcasted_iota(jnp.int32, (rows, size), 0)
    spread = jnp.where(
        row == 0, upper.astype(jnp.float32), jnp.where(row == 1, lower.astype(jnp.float32), 0.0)
    )
    for r in range(NX):
        offset = pl.multiple_of(swapped((x + r) & (NX - 1)) * rows, rows)
        for tap in range(27):
            outs[r][tap] = natural[tap, pl.ds(offset, rows)].astype(outs[r].dtype)
        outs[r][27] = spread.astype(outs[r].dtype)


def call(kernel, where, operands, outs, scratch, flops):
    moved = sum(o.size * o.dtype.itemsize for o in operands)
    moved += sum(math.prod(o.shape) * o.dtype.itemsize for o in outs)
    vmem = pl.BlockSpec(memory_space=pltpu.VMEM)
    return pl.pallas_call(
        kernel,
        out_shape=outs,
        in_specs=[pl.BlockSpec(memory_space=pltpu.SMEM)] + [vmem] * len(operands),
        out_specs=[vmem] * len(outs),
        scratch_shapes=scratch,
        compiler_params=pltpu.CompilerParams(vmem_limit_bytes=VMEM_LIMIT),
        cost_estimate=pl.CostEstimate(flops=flops, bytes_accessed=moved, transcendentals=0),
    )(where, *operands)


def on_device(features, filters, conv_bias, cotangent):
    where = jnp.stack([lax.axis_index("space"), lax.axis_index("chan")]).astype(jnp.int32)
    size, rows = features.shape[-1], filters.shape[0]
    out_size = filters.shape[-1]
    bf16, f32 = jnp.bfloat16, jnp.float32
    shaped = jax.ShapeDtypeStruct

    def along_z(piece, r):
        return permuted(piece, lambda x, q, z: at(x, q, z + r))

    block = permuted(
        filters.transpose(1, 0, 2),
        lambda x, q, z: at(swapped(q % NX), holder((NQ * x + q) // NX), z),
    )
    ahead = permuted(cotangent[0], lambda x, q, z: device(NQ * x + q - 1, z))
    first = permuted(features[1].reshape(FACE, size), lambda x, q, z: at(x, holder(z), z + q))
    second = permuted(
        features[0].reshape(FACE, size), lambda x, q, z: at(x - (q == 0), holder(z), z + q - 1)
    )
    own = jnp.stack([first, second])
    own, block, ahead = lax.optimization_barrier((own, block, ahead))
    blocks = [block] + [
        permuted(block, lambda x, q, z: at(x - shift, q, z)) for shift in range(1, NX)
    ]
    above, below, beyond = along_z(own, -1), along_z(own, 1), along_z(own, 4)
    above, below, beyond, blocks[1], blocks[2] = lax.optimization_barrier(
        (above, below, beyond, blocks[1], blocks[2])
    )
    planes = [
        own,
        above,
        below,
        beyond,
        along_z(jnp.concatenate([above, beyond]), -1),
        along_z(jnp.concatenate([below, beyond]), 1),
    ]

    flops = 2 * 27 * GRID * FACE * size * out_size
    paired_shape = lambda deep, wide: shaped((2, 18 * deep, 2 * wide), bf16)
    columns_shape = shaped((GRID + 2, FACE + 2 * GRID, 3 * size), bf16)
    ahead_weights, back_weights = call(
        weights_kernel,
        where,
        blocks,
        [paired_shape(size, out_size), paired_shape(out_size, size)],
        [pltpu.VMEM((27, size, out_size), bf16)],
        0,
    )
    keep, send, columns = call(
        forward_kernel,
        where,
        planes + [ahead_weights],
        [
            shaped((4, 2, FACE, out_size), f32),
            shaped((4, 2, FACE, out_size), bf16),
            columns_shape,
        ],
        [pltpu.VMEM((NQ, 2, FACE, out_size), f32)],
        flops,
    )
    keep = keep + permuted(send, lambda x, q, z: at(x, q ^ 1, z)).astype(f32)
    pre_act = keep[0]
    for r in range(1, 4):
        pre_act = pre_act + permuted(
            keep[r].astype(bf16), lambda x, q, z: at(x, q + 2 * r, z)
        ).astype(f32)
    pre_act = pre_act + conv_bias[None, None, :]

    target = jnp.stack([cotangent[1], ahead])
    output, slope = gelu_pair(pre_act)
    activated = output.astype(bf16)
    behind = permuted(activated[1], lambda x, q, z: device(NQ * x + q + 1, z))
    activated = jnp.stack([behind, activated[0]])
    grad_pre = (target.reshape(2, FACE, out_size).astype(f32) * slope).astype(bf16)

    slopes = [grad_pre]
    for r in range(1, 4):
        slopes.append(permuted(grad_pre, lambda x, q, z: at(x, q + 2 * r, z)))
    other = [permuted(piece, lambda x, q, z: at(x, q ^ 1, z)) for piece in slopes]
    slopes = slopes + other
    (slope_columns,) = call(slopes_kernel, where, slopes, [columns_shape], [], 0)

    scale = 1.0 / math.sqrt(NX * GRID * FACE)
    terms = call(
        lambda *refs: filters_kernel(scale, *refs),
        where,
        [columns] + slopes,
        [shaped((28, rows, out_size), f32 if r == 0 else bf16) for r in range(NX)],
        [
            pltpu.VMEM((out_size, (GRID + 2) * FACE), bf16),
            pltpu.VMEM((3 * out_size, 9 * size), f32),
            pltpu.VMEM((27, size, out_size), f32),
        ],
        flops,
    )
    where, terms = lax.optimization_barrier((where, terms))
    held = terms[0]
    for r in range(1, NX):
        held = held + permuted(terms[r], lambda x, q, z: at(x + r, q, z)).astype(f32)
    grad_bias = held[27, 0] + held[27, 1]
    held = held[:27].astype(bf16)

    def parts(steps, where, outs):
        return call(
            lambda *refs: backward_kernel(steps, *refs),
            where,
            [slope_columns, back_weights],
            outs,
            [],
            flops * len(steps) // NZ,
        )

    bundle = shaped((4, FACE, size), bf16)
    up, down = parts((2, -3, -2, 3), where, [bundle, bundle])
    up, down, where = lax.optimization_barrier((up, down, where))
    up, down = along_z(up, 1), along_z(down, -1)
    above, below, beyond, summed = parts((1, -1, 4, 0), where, [shaped((2, FACE, size), f32)] * 4)
    up, down, held = lax.optimization_barrier((up, down, held))
    above = (above + up[:2].astype(f32)).astype(bf16)
    below = (below + down[:2].astype(f32)).astype(bf16)
    beyond = (beyond + up[2:].astype(f32) + down[2:].astype(f32)).astype(bf16)
    for piece, r in ((beyond, 4), (above, 1), (below, -1)):
        summed = summed + along_z(piece, r).astype(f32)
    summed = summed.astype(bf16)

    grad_filters = permuted(
        held, lambda x, q, z: device(NX * group(q) + swapped(x), z)
    ).astype(f32)

    def home(half):
        return lambda x, q, z: device(NQ * x + (z - group(q)) % NZ + half, group(q))

    grad_input = jnp.stack([permuted(summed[1], home(1)), permuted(summed[0], home(0))])

    shape = (2, GRID, GRID)
    return (
        activated.reshape(*shape, out_size),
        grad_input.reshape(*shape, size),
        grad_filters.transpose(1, 0, 2),
        grad_bias,
    )


def solution(mesh):
    return jax.shard_map(
        on_device,
        mesh=mesh,
        in_specs=(
            P("space", None, None, "chan"),
            P("space", None, "chan"),
            P("chan"),
            P("space", None, None, "chan"),
        ),
        out_specs=(
            P("space", None, None, "chan"),
            P("space", None, None, "chan"),
            P("space", None, "chan"),
            P("chan"),
        ),
        check_vma=False,
    )
```

```python
import math

import jax
import jax.numpy as jnp
from jax import lax
from jax.experimental import pallas as pl
from jax.experimental.pallas import tpu as pltpu
from jax.sharding import PartitionSpec as P


GRID = 16
FACE = GRID * GRID
NX, NQ, NZ = 4, 8, 8
KAPPA = 0.7978845608028654
CUBIC = 0.044715
VMEM_LIMIT = 24 * 1024 * 1024
Z_STEPS = (0, 1, -1, 4, 2, -3, -2, 3)


def gelu_pair(values):
    inner = KAPPA * (values + CUBIC * values * values * values)
    tangent = jnp.tanh(inner)
    output = 0.5 * values * (1.0 + tangent)
    slope = 0.5 * (1.0 + tangent) + 0.5 * values * (1.0 - tangent * tangent) * KAPPA * (
        1.0 + 3.0 * CUBIC * values * values
    )
    return (output, slope)


def device(space, z):
    return space % (NX * NQ) * NZ + z % NZ


def at(x, q, z):
    return device(x % NX * NQ + q % NQ, z)


def permuted(array, target):
    pairs = [(at(x, q, z), target(x, q, z)) for x in range(NX) for q in range(NQ) for z in range(NZ)]
    return lax.ppermute(array, ("space", "chan"), pairs)


def group(q):
    return q // 2 + 4 * (q % 2)


def holder(group):
    return group % 4 * 2 + group // 4


def swapped(index):
    return index >> 1 | (index & 1) << 1


def position(where):
    space, z = where[0], where[1]
    q = space & (NQ - 1)
    return space >> 3, q, q >> 1, q & 1, z


def ring_pairs(where, steps):
    _, _, y, core, z = position(where)
    return [(z + r - y - 4 * core) & (NQ - 1) for r in steps]


def slope_pairs(where):
    _, _, y, core, _ = position(where)
    rows = [(y - r) & 3 for r in range(4)]
    return [2 * row + core for row in rows] + [2 * row + 1 - core for row in rows]


def store_columns(pairs, planes, columns):
    size = planes[0].shape[-1]
    width = lax.broadcasted_iota(jnp.int32, (FACE, size), 0) % GRID
    rows, whole = columns.shape[1:]
    columns[0] = jnp.zeros((rows, whole), jnp.bfloat16)
    columns[GRID + 1] = jnp.zeros((rows, whole), jnp.bfloat16)
    edge = jnp.zeros((GRID, whole), jnp.bfloat16)
    places = [(ref, 2 * index) for ref in planes for index in range(ref.shape[0] // 2)]
    for pair, (ref, start) in zip(pairs, places):
        for half in range(2):
            depth = 2 * pair + half + 1
            middle = ref[start + half]
            wide = middle.astype(jnp.float32)
            left = jnp.where(width == 0, 0.0, pltpu.roll(wide, 1, 0)).astype(jnp.bfloat16)
            right = jnp.where(width == GRID - 1, 0.0, pltpu.roll(wide, FACE - 1, 0)).astype(
                jnp.bfloat16
            )
            columns[depth, :GRID, :] = edge
            columns[depth, FACE + GRID :, :] = edge
            for c, value in enumerate((left, middle, right)):
                columns[depth, GRID : FACE + GRID, c * size : (c + 1) * size] = value


def window(columns, plane):
    return jnp.concatenate(
        [columns[plane, GRID * b : GRID * b + FACE, :] for b in range(3)], axis=1
    )


def convolved(columns, pairs, paired):
    product = None
    for j in range(2):
        left = jnp.concatenate(
            [
                jnp.concatenate([window(columns, 2 * pair + 2 * j + i) for i in range(2)], axis=1)
                for pair in pairs
            ],
            axis=0,
        )
        part = jnp.dot(left, paired[j], preferred_element_type=jnp.float32)
        product = part if product is None else product + part
    return product


def halves(product, index, size):
    rows = slice(index * FACE, (index + 1) * FACE)
    return [product[rows, o * size : (o + 1) * size] for o in range(2)]


def weights_kernel(where, *refs):
    blocks = refs[:NX]
    ahead, back, natural = refs[NX:]
    size, out_size, rows = natural.shape[1], natural.shape[2], blocks[0].shape[1]
    x = position(where)[0]
    for r in range(NX):
        offset = pl.multiple_of(swapped((x + r) & (NX - 1)) * rows, rows)
        for tap in range(27):
            natural[tap, pl.ds(offset, rows)] = blocks[r][tap]

    def store(ref, a, bc, block):
        height, width = block.shape
        for o in range(2):
            i = a + o
            first = ((i % 2) * 9 + bc) * height
            ref[i // 2, first : first + height, o * width : (o + 1) * width] = block

    for ref, height, width in ((ahead, size, out_size), (back, out_size, size)):
        none = jnp.zeros((9 * height, width), jnp.bfloat16)
        ref[0, : 9 * height, width:] = none
        ref[1, 9 * height :, :width] = none
    for tap in range(27):
        block = natural[tap]
        store(ahead, tap // 9, tap % 9, block)
        turned = block.astype(jnp.float32).T.astype(jnp.bfloat16)
        store(back, (26 - tap) // 9, (26 - tap) % 9, turned)


def forward_kernel(where, *refs):
    *planes, paired, keep, send, columns, total = refs
    size = total.shape[-1]
    _, _, y, core, _ = position(where)
    store_columns(ring_pairs(where, Z_STEPS), planes, columns)

    def step(index, carry):
        product = convolved(columns, [4 * index + p for p in range(4)], paired)
        for p in range(4):
            for o, value in enumerate(halves(product, p, size)):
                total[4 * index + p, o] = value
        return carry

    lax.fori_loop(0, NQ // 4, step, 0)
    for r in range(4):
        row = (y + r) & 3
        for half in range(2):
            keep[r, half] = total[2 * row + core, half]
            send[r, half] = total[2 * row + 1 - core, half].astype(jnp.bfloat16)


def slopes_kernel(where, *refs):
    store_columns(slope_pairs(where), refs[:NQ], refs[NQ])


def backward_kernel(steps, where, columns, paired, *outs):
    product = convolved(columns, ring_pairs(where, steps), paired)
    places = [(out, 2 * index) for out in outs for index in range(out.shape[0] // 2)]
    for index, (out, start) in enumerate(places):
        for half, value in enumerate(halves(product, index, out.shape[-1])):
            out[start + half] = value.astype(out.dtype)


def filters_kernel(scale, where, columns, *refs):
    planes, outs = refs[:NQ], refs[NQ : NQ + NX]
    turned, total, natural = refs[NQ + NX :]
    size, rows = natural.shape[-1], outs[0].shape[1]
    x = position(where)[0]
    turned[:, :FACE] = jnp.zeros((size, FACE), jnp.bfloat16)
    turned[:, (GRID + 1) * FACE :] = jnp.zeros((size, FACE), jnp.bfloat16)
    bias = jnp.zeros((8, size), jnp.float32)
    for pair, ref in zip(slope_pairs(where), planes):
        for half in range(2):
            value = ref[half].astype(jnp.float32)
            bias = bias + jnp.sum(value.reshape(FACE // 8, 8, size), axis=0)
            start = pl.multiple_of((2 * pair + half + 1) * FACE, FACE)
            turned[:, pl.ds(start, FACE)] = value.T.astype(jnp.bfloat16)
    total[...] = jnp.zeros_like(total)

    def step(index, carry):
        first = 8 * index
        left = jnp.concatenate(
            [
                turned[:, pl.ds(pl.multiple_of((first + 2 - a) * FACE, FACE), 8 * FACE)]
                for a in range(3)
            ],
            axis=0,
        )
        right = jnp.concatenate([window(columns, first + 1 + e) for e in range(8)], axis=0)
        total[...] += jnp.dot(left, right, preferred_element_type=jnp.float32)
        return carry

    lax.fori_loop(0, GRID // 8, step, 0)
    for tap in range(27):
        a, bc = tap // 9, tap % 9
        block = total[a * size : (a + 1) * size, bc * size : (bc + 1) * size]
        natural[tap] = block.T * scale
    whole = jnp.sum(bias, axis=0, keepdims=True) * scale
    upper = whole.astype(jnp.bfloat16)
    lower = (whole - upper.astype(jnp.float32)).astype(jnp.bfloat16)
    row = lax.broadcasted_iota(jnp.int32, (rows, size), 0)
    spread = jnp.where(
        row == 0, upper.astype(jnp.float32), jnp.where(row == 1, lower.astype(jnp.float32), 0.0)
    )
    for r in range(NX):
        offset = pl.multiple_of(swapped((x + r) & (NX - 1)) * rows, rows)
        for tap in range(27):
            outs[r][tap] = natural[tap, pl.ds(offset, rows)].astype(outs[r].dtype)
        outs[r][27] = spread.astype(outs[r].dtype)


def call(kernel, where, operands, outs, scratch, flops):
    moved = sum(o.size * o.dtype.itemsize for o in operands)
    moved += sum(math.prod(o.shape) * o.dtype.itemsize for o in outs)
    vmem = pl.BlockSpec(memory_space=pltpu.VMEM)
    return pl.pallas_call(
        kernel,
        out_shape=outs,
        in_specs=[pl.BlockSpec(memory_space=pltpu.SMEM)] + [vmem] * len(operands),
        out_specs=[vmem] * len(outs),
        scratch_shapes=scratch,
        compiler_params=pltpu.CompilerParams(vmem_limit_bytes=VMEM_LIMIT),
        cost_estimate=pl.CostEstimate(flops=flops, bytes_accessed=moved, transcendentals=0),
    )(where, *operands)


def on_device(features, filters, conv_bias, cotangent):
    where = jnp.stack([lax.axis_index("space"), lax.axis_index("chan")]).astype(jnp.int32)
    size, rows = features.shape[-1], filters.shape[0]
    out_size = filters.shape[-1]
    bf16, f32 = jnp.bfloat16, jnp.float32
    shaped = jax.ShapeDtypeStruct

    def along_z(piece, r):
        return permuted(piece, lambda x, q, z: at(x, q, z + r))

    block = permuted(
        filters.transpose(1, 0, 2),
        lambda x, q, z: at(swapped(q % NX), holder((NQ * x + q) // NX), z),
    )
    seconds = permuted(
        jnp.stack([features[0], cotangent[0]]), lambda x, q, z: device(NQ * x + q - 1, z)
    )
    ahead = seconds[1]
    own = jnp.stack([features[1], seconds[0]]).reshape(2, FACE, size)
    own = permuted(own, lambda x, q, z: at(x, holder(z), z + q))
    own, block = lax.optimization_barrier((own, block))
    blocks = [block] + [
        permuted(block, lambda x, q, z: at(x - shift, q, z)) for shift in range(1, NX)
    ]
    above, below, beyond = along_z(own, -1), along_z(own, 1), along_z(own, 4)
    above, below, beyond, blocks[2] = lax.optimization_barrier(
        (above, below, beyond, blocks[2])
    )
    planes = [
        own,
        above,
        below,
        beyond,
        along_z(jnp.concatenate([above, beyond]), -1),
        along_z(jnp.concatenate([below, beyond]), 1),
    ]

    flops = 2 * 27 * GRID * FACE * size * out_size
    paired_shape = lambda deep, wide: shaped((2, 18 * deep, 2 * wide), bf16)
    columns_shape = shaped((GRID + 2, FACE + 2 * GRID, 3 * size), bf16)
    ahead_weights, back_weights = call(
        weights_kernel,
        where,
        blocks,
        [paired_shape(size, out_size), paired_shape(out_size, size)],
        [pltpu.VMEM((27, size, out_size), bf16)],
        0,
    )
    keep, send, columns = call(
        forward_kernel,
        where,
        planes + [ahead_weights],
        [
            shaped((4, 2, FACE, out_size), f32),
            shaped((4, 2, FACE, out_size), bf16),
            columns_shape,
        ],
        [pltpu.VMEM((NQ, 2, FACE, out_size), f32)],
        flops,
    )
    keep = keep + permuted(send, lambda x, q, z: at(x, q ^ 1, z)).astype(f32)
    pre_act = keep[0]
    for r in range(1, 4):
        pre_act = pre_act + permuted(
            keep[r].astype(bf16), lambda x, q, z: at(x, q + 2 * r, z)
        ).astype(f32)
    pre_act = pre_act + conv_bias[None, None, :]

    target = jnp.stack([cotangent[1], ahead])
    output, slope = gelu_pair(pre_act)
    activated = output.astype(bf16)
    behind = permuted(activated[1], lambda x, q, z: device(NQ * x + q + 1, z))
    grad_pre = (target.reshape(2, FACE, out_size).astype(f32) * slope).astype(bf16)

    slopes = [grad_pre]
    for r in range(1, 4):
        slopes.append(permuted(grad_pre, lambda x, q, z: at(x, q + 2 * r, z)))
    other = [permuted(piece, lambda x, q, z: at(x, q ^ 1, z)) for piece in slopes]
    slopes = slopes + other
    (slope_columns,) = call(slopes_kernel, where, slopes, [columns_shape], [], 0)

    scale = 1.0 / math.sqrt(NX * GRID * FACE)
    terms = call(
        lambda *refs: filters_kernel(scale, *refs),
        where,
        [columns] + slopes,
        [shaped((28, rows, out_size), f32 if r == 0 else bf16) for r in range(NX)],
        [
            pltpu.VMEM((out_size, (GRID + 2) * FACE), bf16),
            pltpu.VMEM((3 * out_size, 9 * size), f32),
            pltpu.VMEM((27, size, out_size), f32),
        ],
        flops,
    )
    where, terms, behind = lax.optimization_barrier((where, terms, behind))
    held = terms[0]
    for r in range(1, NX):
        held = held + permuted(terms[r], lambda x, q, z: at(x + r, q, z)).astype(f32)
    grad_bias = held[27, 0] + held[27, 1]
    held = held[:27].astype(bf16)

    def parts(steps, where, outs):
        return call(
            lambda *refs: backward_kernel(steps, *refs),
            where,
            [slope_columns, back_weights],
            outs,
            [],
            flops * len(steps) // NZ,
        )

    bundle = shaped((4, FACE, size), bf16)
    up, down = parts((2, -3, -2, 3), where, [bundle, bundle])
    up, down, where = lax.optimization_barrier((up, down, where))
    up, down = along_z(up, 1), along_z(down, -1)
    above, below, beyond, summed = parts((1, -1, 4, 0), where, [shaped((2, FACE, size), f32)] * 4)
    up, down, held = lax.optimization_barrier((up, down, held))
    above = (above + up[:2].astype(f32)).astype(bf16)
    below = (below + down[:2].astype(f32)).astype(bf16)
    beyond = (beyond + up[2:].astype(f32) + down[2:].astype(f32)).astype(bf16)
    for piece, r in ((beyond, 4), (above, 1), (below, -1)):
        summed = summed + along_z(piece, r).astype(f32)
    summed = summed.astype(bf16)

    grad_filters = permuted(
        held, lambda x, q, z: device(NX * group(q) + swapped(x), z)
    ).astype(f32)

    def home(half):
        return lambda x, q, z: device(NQ * x + (z - group(q)) % NZ + half, group(q))

    grad_input = jnp.stack([permuted(summed[1], home(1)), permuted(summed[0], home(0))])

    activated = jnp.stack([behind, activated[0]])
    shape = (2, GRID, GRID)
    return (
        activated.reshape(*shape, out_size),
        grad_input.reshape(*shape, size),
        grad_filters.transpose(1, 0, 2),
        grad_bias,
    )


def solution(mesh):
    return jax.shard_map(
        on_device,
        mesh=mesh,
        in_specs=(
            P("space", None, None, "chan"),
            P("space", None, "chan"),
            P("chan"),
            P("space", None, None, "chan"),
        ),
        out_specs=(
            P("space", None, None, "chan"),
            P("space", None, None, "chan"),
            P("space", None, "chan"),
            P("chan"),
        ),
        check_vma=False,
    )
```

```python
import math

import jax
import jax.numpy as jnp
from jax import lax
from jax.experimental import pallas as pl
from jax.experimental.pallas import tpu as pltpu
from jax.sharding import PartitionSpec as P


GRID = 16
FACE = GRID * GRID
NX, NQ, NZ = 4, 8, 8
KAPPA = 0.7978845608028654
CUBIC = 0.044715
VMEM_LIMIT = 24 * 1024 * 1024
Z_STEPS = (0, 4, 1, -3, -1, 3, 2, -2)


def gelu_pair(values):
    inner = KAPPA * (values + CUBIC * values * values * values)
    tangent = jnp.tanh(inner)
    output = 0.5 * values * (1.0 + tangent)
    slope = 0.5 * (1.0 + tangent) + 0.5 * values * (1.0 - tangent * tangent) * KAPPA * (
        1.0 + 3.0 * CUBIC * values * values
    )
    return (output, slope)


def device(space, z):
    return space % (NX * NQ) * NZ + z % NZ


def at(x, q, z):
    return device(x % NX * NQ + q % NQ, z)


def permuted(array, target):
    pairs = [(at(x, q, z), target(x, q, z)) for x in range(NX) for q in range(NQ) for z in range(NZ)]
    return lax.ppermute(array, ("space", "chan"), pairs)


def group(q):
    return q // 2 + 4 * (q % 2)


def holder(group):
    return group % 4 * 2 + group // 4


def swapped(index):
    return index >> 1 | (index & 1) << 1


def position(where):
    space, z = where[0], where[1]
    q = space & (NQ - 1)
    return space >> 3, q, q >> 1, q & 1, z


def ring_pairs(where, steps):
    _, _, y, core, z = position(where)
    return [(z + r - y - 4 * core) & (NQ - 1) for r in steps]


def slope_pairs(where):
    _, _, y, core, _ = position(where)
    rows = [(y - r) & 3 for r in range(4)]
    return [2 * row + core for row in rows] + [2 * row + 1 - core for row in rows]


def store_columns(pairs, planes, columns):
    size = planes[0].shape[-1]
    width = lax.broadcasted_iota(jnp.int32, (FACE, size), 0) % GRID
    rows, whole = columns.shape[1:]
    columns[0] = jnp.zeros((rows, whole), jnp.bfloat16)
    columns[GRID + 1] = jnp.zeros((rows, whole), jnp.bfloat16)
    edge = jnp.zeros((GRID, whole), jnp.bfloat16)
    places = [(ref, 2 * index) for ref in planes for index in range(ref.shape[0] // 2)]
    for pair, (ref, start) in zip(pairs, places):
        for half in range(2):
            depth = 2 * pair + half + 1
            middle = ref[start + half]
            wide = middle.astype(jnp.float32)
            left = jnp.where(width == 0, 0.0, pltpu.roll(wide, 1, 0)).astype(jnp.bfloat16)
            right = jnp.where(width == GRID - 1, 0.0, pltpu.roll(wide, FACE - 1, 0)).astype(
                jnp.bfloat16
            )
            columns[depth, :GRID, :] = edge
            columns[depth, FACE + GRID :, :] = edge
            for c, value in enumerate((left, middle, right)):
                columns[depth, GRID : FACE + GRID, c * size : (c + 1) * size] = value


def window(columns, plane):
    return jnp.concatenate(
        [columns[plane, GRID * b : GRID * b + FACE, :] for b in range(3)], axis=1
    )


def convolved(columns, pairs, paired):
    product = None
    for j in range(2):
        left = jnp.concatenate(
            [
                jnp.concatenate([window(columns, 2 * pair + 2 * j + i) for i in range(2)], axis=1)
                for pair in pairs
            ],
            axis=0,
        )
        part = jnp.dot(left, paired[j], preferred_element_type=jnp.float32)
        product = part if product is None else product + part
    return product


def halves(product, index, size):
    rows = slice(index * FACE, (index + 1) * FACE)
    return [product[rows, o * size : (o + 1) * size] for o in range(2)]


def weights_kernel(where, *refs):
    blocks = refs[:NX]
    ahead, back, natural = refs[NX:]
    size, out_size, rows = natural.shape[1], natural.shape[2], blocks[0].shape[1]
    x = position(where)[0]
    for r in range(NX):
        offset = pl.multiple_of(swapped((x + r) & (NX - 1)) * rows, rows)
        for tap in range(27):
            natural[tap, pl.ds(offset, rows)] = blocks[r][tap]

    def store(ref, a, bc, block):
        height, width = block.shape
        for o in range(2):
            i = a + o
            first = ((i % 2) * 9 + bc) * height
            ref[i // 2, first : first + height, o * width : (o + 1) * width] = block

    for ref, height, width in ((ahead, size, out_size), (back, out_size, size)):
        none = jnp.zeros((9 * height, width), jnp.bfloat16)
        ref[0, : 9 * height, width:] = none
        ref[1, 9 * height :, :width] = none
    for tap in range(27):
        block = natural[tap]
        store(ahead, tap // 9, tap % 9, block)
        turned = block.astype(jnp.float32).T.astype(jnp.bfloat16)
        store(back, (26 - tap) // 9, (26 - tap) % 9, turned)


def own_pairs(where):
    _, _, y, core, _ = position(where)
    return [2 * ((y + r) & 3) + core for r in range(4)]


def other_pairs(where):
    _, _, y, core, _ = position(where)
    return [2 * ((y + r) & 3) + 1 - core for r in range(4)]


def slopes_kernel(where, *refs):
    store_columns(slope_pairs(where), refs[:NQ], refs[NQ])


def product_kernel(pairs, where, columns, paired, *outs):
    product = convolved(columns, pairs(where), paired)
    places = [(out, 2 * index) for out in outs for index in range(out.shape[0] // 2)]
    for index, (out, start) in enumerate(places):
        for half, value in enumerate(halves(product, index, out.shape[-1])):
            out[start + half] = value.astype(out.dtype)


def filters_kernel(scale, where, columns, *refs):
    planes, outs = refs[:NQ], refs[NQ : NQ + NX]
    turned, total, natural = refs[NQ + NX :]
    size, rows = natural.shape[-1], outs[0].shape[1]
    x = position(where)[0]
    turned[:, :FACE] = jnp.zeros((size, FACE), jnp.bfloat16)
    turned[:, (GRID + 1) * FACE :] = jnp.zeros((size, FACE), jnp.bfloat16)
    bias = jnp.zeros((8, size), jnp.float32)
    for pair, ref in zip(slope_pairs(where), planes):
        for half in range(2):
            value = ref[half].astype(jnp.float32)
            bias = bias + jnp.sum(value.reshape(FACE // 8, 8, size), axis=0)
            start = pl.multiple_of((2 * pair + half + 1) * FACE, FACE)
            turned[:, pl.ds(start, FACE)] = ref[half].T
    total[...] = jnp.zeros_like(total)

    def step(index, carry):
        first = 8 * index
        left = jnp.concatenate(
            [
                turned[:, pl.ds(pl.multiple_of((first + 2 - a) * FACE, FACE), 8 * FACE)]
                for a in range(3)
            ],
            axis=0,
        )
        right = jnp.concatenate([window(columns, first + 1 + e) for e in range(8)], axis=0)
        total[...] += jnp.dot(left, right, preferred_element_type=jnp.float32)
        return carry

    lax.fori_loop(0, GRID // 8, step, 0)
    for tap in range(27):
        a, bc = tap // 9, tap % 9
        block = total[a * size : (a + 1) * size, bc * size : (bc + 1) * size]
        natural[tap] = (block * scale).astype(jnp.bfloat16).T
    whole = jnp.sum(bias, axis=0, keepdims=True) * scale
    upper = whole.astype(jnp.bfloat16)
    lower = (whole - upper.astype(jnp.float32)).astype(jnp.bfloat16)
    row = lax.broadcasted_iota(jnp.int32, (rows, size), 0)
    spread = jnp.where(
        row == 0, upper.astype(jnp.float32), jnp.where(row == 1, lower.astype(jnp.float32), 0.0)
    )
    for r in range(NX):
        offset = pl.multiple_of(swapped((x + r) & (NX - 1)) * rows, rows)
        for tap in range(27):
            outs[r][tap] = natural[tap, pl.ds(offset, rows)]
        outs[r][27] = spread.astype(outs[r].dtype)


def call(kernel, where, operands, outs, scratch, flops):
    moved = sum(o.size * o.dtype.itemsize for o in operands)
    moved += sum(math.prod(o.shape) * o.dtype.itemsize for o in outs)
    vmem = pl.BlockSpec(memory_space=pltpu.VMEM)
    return pl.pallas_call(
        kernel,
        out_shape=outs,
        in_specs=[pl.BlockSpec(memory_space=pltpu.SMEM)] + [vmem] * len(operands),
        out_specs=[vmem] * len(outs),
        scratch_shapes=scratch,
        compiler_params=pltpu.CompilerParams(vmem_limit_bytes=VMEM_LIMIT),
        cost_estimate=pl.CostEstimate(flops=flops, bytes_accessed=moved, transcendentals=0),
    )(where, *operands)


def on_device(features, filters, conv_bias, cotangent):
    where = jnp.stack([lax.axis_index("space"), lax.axis_index("chan")]).astype(jnp.int32)
    size, rows = features.shape[-1], filters.shape[0]
    out_size = filters.shape[-1]
    bf16, f32 = jnp.bfloat16, jnp.float32
    shaped = jax.ShapeDtypeStruct

    def along_z(piece, r):
        return permuted(piece, lambda x, q, z: at(x, q, z + r))

    block = permuted(
        filters.transpose(1, 0, 2),
        lambda x, q, z: at(swapped(q % NX), holder((NQ * x + q) // NX), z),
    )
    seconds = permuted(
        jnp.stack([features[0], cotangent[0]]), lambda x, q, z: device(NQ * x + q - 1, z)
    )
    ahead = seconds[1]
    own = jnp.stack([features[1], seconds[0]]).reshape(2, FACE, size)
    own = jnp.concatenate(
        [permuted(own, lambda x, q, z: at(x, holder(z), z + q + step)) for step in (0, 4)]
    )
    blocks = [block] + [
        permuted(block, lambda x, q, z: at(x - shift, q, z)) for shift in range(1, NX)
    ]
    above, below = along_z(own, -1), along_z(own, 1)
    above, below, block = lax.optimization_barrier((above, below, block))
    planes = [own, above, below, along_z(above[:2], -1), along_z(below[:2], 1)]

    flops = 2 * 27 * GRID * FACE * size * out_size
    paired_shape = lambda deep, wide: shaped((2, 18 * deep, 2 * wide), bf16)
    columns_shape = shaped((GRID + 2, FACE + 2 * GRID, 3 * size), bf16)
    (columns,) = call(
        lambda where, *refs: store_columns(ring_pairs(where, Z_STEPS), refs[:-1], refs[-1]),
        where,
        planes,
        [columns_shape],
        [],
        0,
    )
    columns, blocks[1], blocks[3] = lax.optimization_barrier((columns, blocks[1], blocks[3]))
    ahead_weights, back_weights = call(
        weights_kernel,
        where,
        blocks,
        [paired_shape(size, out_size), paired_shape(out_size, size)],
        [pltpu.VMEM((27, size, out_size), bf16)],
        0,
    )
    def products(pairs, where, columns, weights, outs):
        return call(
            lambda *refs: product_kernel(pairs, *refs),
            where,
            [columns, weights],
            outs,
            [],
            flops // 2,
        )

    (send,) = products(other_pairs, where, columns, ahead_weights, [shaped((8, FACE, out_size), bf16)])
    where, send = lax.optimization_barrier((where, send))
    send = permuted(send, lambda x, q, z: at(x, q ^ 1, z)).astype(f32)
    keep = products(own_pairs, where, columns, ahead_weights, [shaped((2, FACE, out_size), f32)] * 4)
    keep = [piece + send[2 * r : 2 * r + 2] for r, piece in enumerate(keep)]
    pre_act = keep[0]
    for r in range(1, 4):
        pre_act = pre_act + permuted(
            keep[r].astype(bf16), lambda x, q, z: at(x, q + 2 * r, z)
        ).astype(f32)
    pre_act = pre_act + conv_bias[None, None, :]

    target = jnp.stack([cotangent[1], ahead])
    output, slope = gelu_pair(pre_act)
    activated = output.astype(bf16)
    grad_pre = (target.reshape(2, FACE, out_size).astype(f32) * slope).astype(bf16)

    slopes = [grad_pre]
    for r in range(1, 4):
        slopes.append(permuted(grad_pre, lambda x, q, z: at(x, q + 2 * r, z)))
    other = [permuted(piece, lambda x, q, z: at(x, q ^ 1, z)) for piece in slopes]
    slopes = slopes + other
    (slope_columns,) = call(slopes_kernel, where, slopes, [columns_shape], [], 0)

    scale = 1.0 / math.sqrt(NX * GRID * FACE)
    terms = call(
        lambda *refs: filters_kernel(scale, *refs),
        where,
        [columns] + slopes,
        [shaped((28, rows, out_size), bf16)] * NX,
        [
            pltpu.VMEM((out_size, (GRID + 2) * FACE), bf16),
            pltpu.VMEM((3 * out_size, 9 * size), f32),
            pltpu.VMEM((27, size, out_size), bf16),
        ],
        flops,
    )
    where, terms = lax.optimization_barrier((where, terms))
    held = terms[0].astype(f32)
    for r in range(1, NX):
        held = held + permuted(terms[r], lambda x, q, z: at(x + r, q, z)).astype(f32)
    grad_bias = held[27, 0] + held[27, 1]
    held = held[:27].astype(bf16)

    def parts(steps, where, kinds):
        return call(
            lambda *refs: product_kernel(lambda where: ring_pairs(where, steps), *refs),
            where,
            [slope_columns, back_weights],
            [shaped((2, FACE, size), kind) for kind in kinds],
            [],
            flops * len(steps) // NZ,
        )

    up, down = parts((2, -2), where, [bf16, bf16])
    up, down, where = lax.optimization_barrier((up, down, where))
    up, down = along_z(up, 1).astype(f32), along_z(down, -1).astype(f32)
    above, far_above, below, far_below = parts((1, -3, -1, 3), where, [f32, bf16, f32, bf16])
    above, below, where = lax.optimization_barrier((above, below, where))
    above = jnp.concatenate([(above + up).astype(bf16), far_above])
    below = jnp.concatenate([(below + down).astype(bf16), far_below])
    above, below, held = lax.optimization_barrier((above, below, held))
    near, beyond = parts((0, 4), where, [f32, f32])
    above, below = along_z(above, 1).astype(f32), along_z(below, -1).astype(f32)
    near = (near + above[:2] + below[:2]).astype(bf16)
    beyond = (beyond + above[2:] + below[2:]).astype(bf16)

    grad_filters = permuted(
        held, lambda x, q, z: device(NX * group(q) + swapped(x), z)
    ).astype(f32)

    def home(step):
        return lambda x, q, z: device(NQ * x + (z - group(q) - step) % NZ, group(q))

    near, beyond = permuted(near, home(0)).astype(f32), permuted(beyond, home(4)).astype(f32)
    summed = (near + beyond).astype(bf16)
    seconds = permuted(
        jnp.stack([activated[1], summed[1]]), lambda x, q, z: device(NQ * x + q + 1, z)
    )
    activated = jnp.stack([seconds[0], activated[0]])
    grad_input = jnp.stack([seconds[1], summed[0]])

    shape = (2, GRID, GRID)
    return (
        activated.reshape(*shape, out_size),
        grad_input.reshape(*shape, size),
        grad_filters.transpose(1, 0, 2),
        grad_bias,
    )


def solution(mesh):
    return jax.shard_map(
        on_device,
        mesh=mesh,
        in_specs=(
            P("space", None, None, "chan"),
            P("space", None, "chan"),
            P("chan"),
            P("space", None, None, "chan"),
        ),
        out_specs=(
            P("space", None, None, "chan"),
            P("space", None, None, "chan"),
            P("space", None, "chan"),
            P("chan"),
        ),
        check_vma=False,
    )
```

```python
import math

import jax
import jax.numpy as jnp
from jax import lax
from jax.experimental import pallas as pl
from jax.experimental.pallas import tpu as pltpu
from jax.sharding import PartitionSpec as P


GRID = 16
FACE = GRID * GRID
NX, NQ, NZ = 4, 8, 8
KAPPA = 0.7978845608028654
CUBIC = 0.044715
VMEM_LIMIT = 24 * 1024 * 1024
Z_STEPS = (0, 4, 1, -3, -1, 3, 2, -2)


def gelu_pair(values):
    inner = KAPPA * (values + CUBIC * values * values * values)
    tangent = jnp.tanh(inner)
    output = 0.5 * values * (1.0 + tangent)
    slope = 0.5 * (1.0 + tangent) + 0.5 * values * (1.0 - tangent * tangent) * KAPPA * (
        1.0 + 3.0 * CUBIC * values * values
    )
    return (output, slope)


def device(space, z):
    return space % (NX * NQ) * NZ + z % NZ


def at(x, q, z):
    return device(x % NX * NQ + q % NQ, z)


def permuted(array, target):
    pairs = [(at(x, q, z), target(x, q, z)) for x in range(NX) for q in range(NQ) for z in range(NZ)]
    return lax.ppermute(array, ("space", "chan"), pairs)


def group(q):
    return q // 2 + 4 * (q % 2)


def holder(group):
    return group % 4 * 2 + group // 4


def swapped(index):
    return index >> 1 | (index & 1) << 1


def position(where):
    space, z = where[0], where[1]
    q = space & (NQ - 1)
    return space >> 3, q, q >> 1, q & 1, z


def ring_pairs(where, steps):
    _, _, y, core, z = position(where)
    return [(z + r - y - 4 * core) & (NQ - 1) for r in steps]


def slope_pairs(where):
    _, _, y, core, _ = position(where)
    rows = [(y - r) & 3 for r in range(4)]
    return [2 * row + core for row in rows] + [2 * row + 1 - core for row in rows]


def store_columns(pairs, planes, columns):
    size = planes[0].shape[-1]
    width = lax.broadcasted_iota(jnp.int32, (FACE, size), 0) % GRID
    rows, whole = columns.shape[1:]
    columns[0] = jnp.zeros((rows, whole), jnp.bfloat16)
    columns[GRID + 1] = jnp.zeros((rows, whole), jnp.bfloat16)
    edge = jnp.zeros((GRID, whole), jnp.bfloat16)
    places = [(ref, 2 * index) for ref in planes for index in range(ref.shape[0] // 2)]
    for pair, (ref, start) in zip(pairs, places):
        for half in range(2):
            depth = 2 * pair + half + 1
            middle = ref[start + half]
            wide = middle.astype(jnp.float32)
            left = jnp.where(width == 0, 0.0, pltpu.roll(wide, 1, 0)).astype(jnp.bfloat16)
            right = jnp.where(width == GRID - 1, 0.0, pltpu.roll(wide, FACE - 1, 0)).astype(
                jnp.bfloat16
            )
            columns[depth, :GRID, :] = edge
            columns[depth, FACE + GRID :, :] = edge
            for c, value in enumerate((left, middle, right)):
                columns[depth, GRID : FACE + GRID, c * size : (c + 1) * size] = value


def window(columns, plane):
    return jnp.concatenate(
        [columns[plane, GRID * b : GRID * b + FACE, :] for b in range(3)], axis=1
    )


def convolved(columns, pairs, paired):
    product = None
    for j in range(2):
        left = jnp.concatenate(
            [
                jnp.concatenate([window(columns, 2 * pair + 2 * j + i) for i in range(2)], axis=1)
                for pair in pairs
            ],
            axis=0,
        )
        part = jnp.dot(left, paired[j], preferred_element_type=jnp.float32)
        product = part if product is None else product + part
    return product


def halves(product, index, size):
    rows = slice(index * FACE, (index + 1) * FACE)
    return [product[rows, o * size : (o + 1) * size] for o in range(2)]


def weights_kernel(where, *refs):
    blocks = refs[:NX]
    ahead, back, natural = refs[NX:]
    size, out_size, rows = natural.shape[1], natural.shape[2], blocks[0].shape[1]
    x = position(where)[0]
    for r in range(NX):
        offset = pl.multiple_of(swapped((x + r) & (NX - 1)) * rows, rows)
        for tap in range(27):
            natural[tap, pl.ds(offset, rows)] = blocks[r][tap]

    def store(ref, a, bc, block):
        height, width = block.shape
        for o in range(2):
            i = a + o
            first = ((i % 2) * 9 + bc) * height
            ref[i // 2, first : first + height, o * width : (o + 1) * width] = block

    for ref, height, width in ((ahead, size, out_size), (back, out_size, size)):
        none = jnp.zeros((9 * height, width), jnp.bfloat16)
        ref[0, : 9 * height, width:] = none
        ref[1, 9 * height :, :width] = none
    for tap in range(27):
        block = natural[tap]
        store(ahead, tap // 9, tap % 9, block)
        turned = block.astype(jnp.float32).T.astype(jnp.bfloat16)
        store(back, (26 - tap) // 9, (26 - tap) % 9, turned)


def own_pairs(where):
    _, _, y, core, _ = position(where)
    return [2 * ((y + r) & 3) + core for r in range(4)]


def other_pairs(where):
    _, _, y, core, _ = position(where)
    return [2 * ((y + r) & 3) + 1 - core for r in range(4)]


def slopes_kernel(where, *refs):
    store_columns(slope_pairs(where), refs[:NQ], refs[NQ])


def product_kernel(pairs, where, columns, paired, *outs):
    product = convolved(columns, pairs(where), paired)
    places = [(out, 2 * index) for out in outs for index in range(out.shape[0] // 2)]
    for index, (out, start) in enumerate(places):
        for half, value in enumerate(halves(product, index, out.shape[-1])):
            out[start + half] = value.astype(out.dtype)


def filters_kernel(scale, where, columns, *refs):
    planes, outs = refs[:NQ], refs[NQ : NQ + NX]
    turned, total, natural = refs[NQ + NX :]
    size, rows = natural.shape[-1], outs[0].shape[1]
    x = position(where)[0]
    turned[:, :FACE] = jnp.zeros((size, FACE), jnp.bfloat16)
    turned[:, (GRID + 1) * FACE :] = jnp.zeros((size, FACE), jnp.bfloat16)
    bias = jnp.zeros((8, size), jnp.float32)
    for pair, ref in zip(slope_pairs(where), planes):
        for half in range(2):
            value = ref[half].astype(jnp.float32)
            bias = bias + jnp.sum(value.reshape(FACE // 8, 8, size), axis=0)
            start = pl.multiple_of((2 * pair + half + 1) * FACE, FACE)
            turned[:, pl.ds(start, FACE)] = ref[half].T
    total[...] = jnp.zeros_like(total)

    def step(index, carry):
        first = 8 * index
        left = jnp.concatenate(
            [
                turned[:, pl.ds(pl.multiple_of((first + 2 - a) * FACE, FACE), 8 * FACE)]
                for a in range(3)
            ],
            axis=0,
        )
        right = jnp.concatenate([window(columns, first + 1 + e) for e in range(8)], axis=0)
        total[...] += jnp.dot(left, right, preferred_element_type=jnp.float32)
        return carry

    lax.fori_loop(0, GRID // 8, step, 0)
    for tap in range(27):
        a, bc = tap // 9, tap % 9
        block = total[a * size : (a + 1) * size, bc * size : (bc + 1) * size]
        natural[tap] = (block * scale).astype(jnp.bfloat16).T
    whole = jnp.sum(bias, axis=0, keepdims=True) * scale
    upper = whole.astype(jnp.bfloat16)
    lower = (whole - upper.astype(jnp.float32)).astype(jnp.bfloat16)
    row = lax.broadcasted_iota(jnp.int32, (rows, size), 0)
    spread = jnp.where(
        row == 0, upper.astype(jnp.float32), jnp.where(row == 1, lower.astype(jnp.float32), 0.0)
    )
    for r in range(NX):
        offset = pl.multiple_of(swapped((x + r) & (NX - 1)) * rows, rows)
        for tap in range(27):
            outs[r][tap] = natural[tap, pl.ds(offset, rows)]
        outs[r][27] = spread.astype(outs[r].dtype)


def call(kernel, where, operands, outs, scratch, flops):
    moved = sum(o.size * o.dtype.itemsize for o in operands)
    moved += sum(math.prod(o.shape) * o.dtype.itemsize for o in outs)
    vmem = pl.BlockSpec(memory_space=pltpu.VMEM)
    return pl.pallas_call(
        kernel,
        out_shape=outs,
        in_specs=[pl.BlockSpec(memory_space=pltpu.SMEM)] + [vmem] * len(operands),
        out_specs=[vmem] * len(outs),
        scratch_shapes=scratch,
        compiler_params=pltpu.CompilerParams(vmem_limit_bytes=VMEM_LIMIT),
        cost_estimate=pl.CostEstimate(flops=flops, bytes_accessed=moved, transcendentals=0),
    )(where, *operands)


def on_device(features, filters, conv_bias, cotangent):
    where = jnp.stack([lax.axis_index("space"), lax.axis_index("chan")]).astype(jnp.int32)
    size, rows = features.shape[-1], filters.shape[0]
    out_size = filters.shape[-1]
    bf16, f32 = jnp.bfloat16, jnp.float32
    shaped = jax.ShapeDtypeStruct

    def along_z(piece, r):
        return permuted(piece, lambda x, q, z: at(x, q, z + r))

    block = permuted(
        filters.transpose(1, 0, 2),
        lambda x, q, z: at(swapped(q % NX), holder((NQ * x + q) // NX), z),
    )
    seconds = permuted(
        jnp.stack([features[0], cotangent[0]]), lambda x, q, z: device(NQ * x + q - 1, z)
    )
    ahead = seconds[1]
    own = jnp.stack([features[1], seconds[0]]).reshape(2, FACE, size)
    own = jnp.concatenate(
        [permuted(own, lambda x, q, z: at(x, holder(z), z + q + step)) for step in (0, 4)]
    )
    blocks = [block] + [
        permuted(block, lambda x, q, z: at(x - shift, q, z)) for shift in range(1, NX)
    ]
    above, below = along_z(own, -1), along_z(own, 1)
    above, below, block = lax.optimization_barrier((above, below, block))
    planes = [own, above, below, along_z(above[:2], -1), along_z(below[:2], 1)]

    flops = 2 * 27 * GRID * FACE * size * out_size
    paired_shape = lambda deep, wide: shaped((2, 18 * deep, 2 * wide), bf16)
    columns_shape = shaped((GRID + 2, FACE + 2 * GRID, 3 * size), bf16)
    (columns,) = call(
        lambda where, *refs: store_columns(ring_pairs(where, Z_STEPS), refs[:-1], refs[-1]),
        where,
        planes,
        [columns_shape],
        [],
        0,
    )
    columns, blocks[1], blocks[3] = lax.optimization_barrier((columns, blocks[1], blocks[3]))
    ahead_weights, back_weights = call(
        weights_kernel,
        where,
        blocks,
        [paired_shape(size, out_size), paired_shape(out_size, size)],
        [pltpu.VMEM((27, size, out_size), bf16)],
        0,
    )
    def products(pairs, where, columns, weights, outs):
        return call(
            lambda *refs: product_kernel(pairs, *refs),
            where,
            [columns, weights],
            outs,
            [],
            flops // 2,
        )

    (send,) = products(other_pairs, where, columns, ahead_weights, [shaped((8, FACE, out_size), bf16)])
    where, send = lax.optimization_barrier((where, send))
    send = permuted(send, lambda x, q, z: at(x, q ^ 1, z)).astype(f32)
    keep = products(own_pairs, where, columns, ahead_weights, [shaped((2, FACE, out_size), f32)] * 4)
    keep = [piece + send[2 * r : 2 * r + 2] for r, piece in enumerate(keep)]
    pre_act = keep[0]
    for r in (2, 1, 3):
        pre_act = pre_act + permuted(
            keep[r].astype(bf16), lambda x, q, z: at(x, q + 2 * r, z)
        ).astype(f32)
    pre_act = pre_act + conv_bias[None, None, :]

    target = jnp.stack([cotangent[1], ahead])
    output, slope = gelu_pair(pre_act)
    activated = output.astype(bf16)
    grad_pre = (target.reshape(2, FACE, out_size).astype(f32) * slope).astype(bf16)

    slopes = [grad_pre]
    for r in range(1, 4):
        slopes.append(permuted(grad_pre, lambda x, q, z: at(x, q + 2 * r, z)))
    other = [permuted(piece, lambda x, q, z: at(x, q ^ 1, z)) for piece in slopes]
    slopes = slopes + other
    (slope_columns,) = call(slopes_kernel, where, slopes, [columns_shape], [], 0)

    scale = 1.0 / math.sqrt(NX * GRID * FACE)
    terms = call(
        lambda *refs: filters_kernel(scale, *refs),
        where,
        [columns] + slopes,
        [shaped((28, rows, out_size), bf16)] * NX,
        [
            pltpu.VMEM((out_size, (GRID + 2) * FACE), bf16),
            pltpu.VMEM((3 * out_size, 9 * size), f32),
            pltpu.VMEM((27, size, out_size), bf16),
        ],
        flops,
    )
    where, terms = lax.optimization_barrier((where, terms))
    held = terms[0].astype(f32)
    for r in range(1, NX):
        held = held + permuted(terms[r], lambda x, q, z: at(x + r, q, z)).astype(f32)
    grad_bias = held[27, 0] + held[27, 1]
    held = held[:27].astype(bf16)

    def parts(steps, where, kinds):
        return call(
            lambda *refs: product_kernel(lambda where: ring_pairs(where, steps), *refs),
            where,
            [slope_columns, back_weights],
            [shaped((2, FACE, size), kind) for kind in kinds],
            [],
            flops * len(steps) // NZ,
        )

    up, down = parts((2, -2), where, [bf16, bf16])
    up, down, where = lax.optimization_barrier((up, down, where))
    up, down = along_z(up, 1).astype(f32), along_z(down, -1).astype(f32)
    above, far_above, below, far_below = parts((1, -3, -1, 3), where, [f32, bf16, f32, bf16])
    above, below, where = lax.optimization_barrier((above, below, where))
    above = jnp.concatenate([(above + up).astype(bf16), far_above])
    below = jnp.concatenate([(below + down).astype(bf16), far_below])
    above, below, where = lax.optimization_barrier((above, below, where))
    near, beyond = parts((0, 4), where, [f32, f32])
    above, below = along_z(above, 1).astype(f32), along_z(below, -1).astype(f32)
    near = (near + above[:2] + below[:2]).astype(bf16)
    beyond = (beyond + above[2:] + below[2:]).astype(bf16)

    near, beyond, held, activated = lax.optimization_barrier((near, beyond, held, activated))

    def next_slab(plane):
        return permuted(plane, lambda x, q, z: device(NQ * x + q + 1, z))

    def home(step):
        return lambda x, q, z: device(NQ * x + (z - group(q) - step) % NZ, group(q))

    near, beyond = permuted(near, home(0)).astype(f32), permuted(beyond, home(4)).astype(f32)
    summed = (near + beyond).astype(bf16)
    grad_filters = permuted(
        held, lambda x, q, z: device(NX * group(q) + swapped(x), z)
    ).astype(f32)

    activated = jnp.stack([next_slab(activated[1]), activated[0]])
    grad_input = jnp.stack([next_slab(summed[1]), summed[0]])
    shape = (2, GRID, GRID)
    return (
        activated.reshape(*shape, out_size),
        grad_input.reshape(*shape, size),
        grad_filters.transpose(1, 0, 2),
        grad_bias,
    )


def solution(mesh):
    return jax.shard_map(
        on_device,
        mesh=mesh,
        in_specs=(
            P("space", None, None, "chan"),
            P("space", None, "chan"),
            P("chan"),
            P("space", None, None, "chan"),
        ),
        out_specs=(
            P("space", None, None, "chan"),
            P("space", None, None, "chan"),
            P("space", None, "chan"),
            P("chan"),
        ),
        check_vma=False,
    )
```

```python
import math

import jax
import jax.numpy as jnp
from jax import lax
from jax.experimental import pallas as pl
from jax.experimental.pallas import tpu as pltpu
from jax.sharding import PartitionSpec as P


GRID = 16
FACE = GRID * GRID
NX, NQ, NZ = 4, 8, 8
KAPPA = 0.7978845608028654
CUBIC = 0.044715
VMEM_LIMIT = 24 * 1024 * 1024
Z_STEPS = (0, 4, 1, -3, -1, 3, 2, -2)


def gelu_pair(values):
    inner = KAPPA * (values + CUBIC * values * values * values)
    tangent = jnp.tanh(inner)
    output = 0.5 * values * (1.0 + tangent)
    slope = 0.5 * (1.0 + tangent) + 0.5 * values * (1.0 - tangent * tangent) * KAPPA * (
        1.0 + 3.0 * CUBIC * values * values
    )
    return (output, slope)


def device(space, z):
    return space % (NX * NQ) * NZ + z % NZ


def at(x, q, z):
    return device(x % NX * NQ + q % NQ, z)


def permuted(array, target):
    pairs = [(at(x, q, z), target(x, q, z)) for x in range(NX) for q in range(NQ) for z in range(NZ)]
    return lax.ppermute(array, ("space", "chan"), pairs)


def group(q):
    return q // 2 + 4 * (q % 2)


def holder(group):
    return group % 4 * 2 + group // 4


def swapped(index):
    return index >> 1 | (index & 1) << 1


def position(where):
    space, z = where[0], where[1]
    q = space & (NQ - 1)
    return space >> 3, q, q >> 1, q & 1, z


def ring_pairs(where, steps):
    _, _, y, core, z = position(where)
    return [(z + r - y - 4 * core) & (NQ - 1) for r in steps]


def slope_pairs(where):
    _, _, y, core, _ = position(where)
    rows = [(y - r) & 3 for r in range(4)]
    return [2 * row + core for row in rows] + [2 * row + 1 - core for row in rows]


def store_columns(pairs, planes, columns):
    size = planes[0].shape[-1]
    width = lax.broadcasted_iota(jnp.int32, (FACE, size), 0) % GRID
    rows, whole = columns.shape[1:]
    columns[0] = jnp.zeros((rows, whole), jnp.bfloat16)
    columns[GRID + 1] = jnp.zeros((rows, whole), jnp.bfloat16)
    edge = jnp.zeros((GRID, whole), jnp.bfloat16)
    places = [(ref, 2 * index) for ref in planes for index in range(ref.shape[0] // 2)]
    for pair, (ref, start) in zip(pairs, places):
        for half in range(2):
            depth = 2 * pair + half + 1
            middle = ref[start + half]
            wide = middle.astype(jnp.float32)
            left = jnp.where(width == 0, 0.0, pltpu.roll(wide, 1, 0)).astype(jnp.bfloat16)
            right = jnp.where(width == GRID - 1, 0.0, pltpu.roll(wide, FACE - 1, 0)).astype(
                jnp.bfloat16
            )
            columns[depth, :GRID, :] = edge
            columns[depth, FACE + GRID :, :] = edge
            for c, value in enumerate((left, middle, right)):
                columns[depth, GRID : FACE + GRID, c * size : (c + 1) * size] = value


def window(columns, plane):
    return jnp.concatenate(
        [columns[plane, GRID * b : GRID * b + FACE, :] for b in range(3)], axis=1
    )


def convolved(columns, pairs, paired):
    product = None
    for j in range(2):
        left = jnp.concatenate(
            [
                jnp.concatenate([window(columns, 2 * pair + 2 * j + i) for i in range(2)], axis=1)
                for pair in pairs
            ],
            axis=0,
        )
        part = jnp.dot(left, paired[j], preferred_element_type=jnp.float32)
        product = part if product is None else product + part
    return product


def halves(product, index, size):
    rows = slice(index * FACE, (index + 1) * FACE)
    return [product[rows, o * size : (o + 1) * size] for o in range(2)]


def weights_kernel(where, *refs):
    blocks = refs[:NX]
    ahead, back, natural = refs[NX:]
    size, out_size, rows = natural.shape[1], natural.shape[2], blocks[0].shape[1]
    x = position(where)[0]
    for r in range(NX):
        offset = pl.multiple_of(swapped((x + r) & (NX - 1)) * rows, rows)
        for tap in range(27):
            natural[tap, pl.ds(offset, rows)] = blocks[r][tap]

    def store(ref, a, bc, block):
        height, width = block.shape
        for o in range(2):
            i = a + o
            first = ((i % 2) * 9 + bc) * height
            ref[i // 2, first : first + height, o * width : (o + 1) * width] = block

    for ref, height, width in ((ahead, size, out_size), (back, out_size, size)):
        none = jnp.zeros((9 * height, width), jnp.bfloat16)
        ref[0, : 9 * height, width:] = none
        ref[1, 9 * height :, :width] = none
    for tap in range(27):
        block = natural[tap]
        store(ahead, tap // 9, tap % 9, block)
        turned = block.astype(jnp.float32).T.astype(jnp.bfloat16)
        store(back, (26 - tap) // 9, (26 - tap) % 9, turned)


def own_pairs(where):
    _, _, y, core, _ = position(where)
    return [2 * ((y + r) & 3) + core for r in range(4)]


def other_pairs(where):
    _, _, y, core, _ = position(where)
    return [2 * ((y + r) & 3) + 1 - core for r in range(4)]


def slopes_kernel(where, *refs):
    store_columns(slope_pairs(where), refs[:NQ], refs[NQ])


def product_kernel(pairs, where, columns, paired, *outs):
    product = convolved(columns, pairs(where), paired)
    places = [(out, 2 * index) for out in outs for index in range(out.shape[0] // 2)]
    for index, (out, start) in enumerate(places):
        for half, value in enumerate(halves(product, index, out.shape[-1])):
            out[start + half] = value.astype(out.dtype)


def filters_kernel(scale, where, columns, *refs):
    planes, outs = refs[:NQ], refs[NQ : NQ + NX]
    turned, total, natural = refs[NQ + NX :]
    size, rows = natural.shape[-1], outs[0].shape[1]
    x = position(where)[0]
    turned[:, :FACE] = jnp.zeros((size, FACE), jnp.bfloat16)
    turned[:, (GRID + 1) * FACE :] = jnp.zeros((size, FACE), jnp.bfloat16)
    bias = jnp.zeros((8, size), jnp.float32)
    for pair, ref in zip(slope_pairs(where), planes):
        for half in range(2):
            value = ref[half].astype(jnp.float32)
            bias = bias + jnp.sum(value.reshape(FACE // 8, 8, size), axis=0)
            start = pl.multiple_of((2 * pair + half + 1) * FACE, FACE)
            turned[:, pl.ds(start, FACE)] = ref[half].T
    total[...] = jnp.zeros_like(total)

    def step(index, carry):
        first = 8 * index
        left = jnp.concatenate(
            [
                turned[:, pl.ds(pl.multiple_of((first + 2 - a) * FACE, FACE), 8 * FACE)]
                for a in range(3)
            ],
            axis=0,
        )
        right = jnp.concatenate([window(columns, first + 1 + e) for e in range(8)], axis=0)
        total[...] += jnp.dot(left, right, preferred_element_type=jnp.float32)
        return carry

    lax.fori_loop(0, GRID // 8, step, 0)
    for tap in range(27):
        a, bc = tap // 9, tap % 9
        block = total[a * size : (a + 1) * size, bc * size : (bc + 1) * size]
        natural[tap] = (block * scale).astype(jnp.bfloat16).T
    whole = jnp.sum(bias, axis=0, keepdims=True) * scale
    upper = whole.astype(jnp.bfloat16)
    lower = (whole - upper.astype(jnp.float32)).astype(jnp.bfloat16)
    row = lax.broadcasted_iota(jnp.int32, (rows, size), 0)
    spread = jnp.where(
        row == 0, upper.astype(jnp.float32), jnp.where(row == 1, lower.astype(jnp.float32), 0.0)
    )
    for r in range(NX):
        offset = pl.multiple_of(swapped((x + r) & (NX - 1)) * rows, rows)
        for tap in range(27):
            outs[r][tap] = natural[tap, pl.ds(offset, rows)]
        outs[r][27] = spread.astype(outs[r].dtype)


def call(kernel, where, operands, outs, scratch, flops):
    moved = sum(o.size * o.dtype.itemsize for o in operands)
    moved += sum(math.prod(o.shape) * o.dtype.itemsize for o in outs)
    vmem = pl.BlockSpec(memory_space=pltpu.VMEM)
    return pl.pallas_call(
        kernel,
        out_shape=outs,
        in_specs=[pl.BlockSpec(memory_space=pltpu.SMEM)] + [vmem] * len(operands),
        out_specs=[vmem] * len(outs),
        scratch_shapes=scratch,
        compiler_params=pltpu.CompilerParams(vmem_limit_bytes=VMEM_LIMIT),
        cost_estimate=pl.CostEstimate(flops=flops, bytes_accessed=moved, transcendentals=0),
    )(where, *operands)


def on_device(features, filters, conv_bias, cotangent):
    where = jnp.stack([lax.axis_index("space"), lax.axis_index("chan")]).astype(jnp.int32)
    size, rows = features.shape[-1], filters.shape[0]
    out_size = filters.shape[-1]
    bf16, f32 = jnp.bfloat16, jnp.float32
    shaped = jax.ShapeDtypeStruct

    def along_z(piece, r):
        return permuted(piece, lambda x, q, z: at(x, q, z + r))

    block = permuted(
        filters.transpose(1, 0, 2),
        lambda x, q, z: at(swapped(q % NX), holder((NQ * x + q) // NX), z),
    )
    seconds = permuted(
        jnp.stack([features[0], cotangent[0]]), lambda x, q, z: device(NQ * x + q - 1, z)
    )
    ahead = seconds[1]
    own = jnp.stack([features[1], seconds[0]]).reshape(2, FACE, size)
    own = jnp.concatenate(
        [permuted(own, lambda x, q, z: at(x, holder(z), z + q + step)) for step in (0, 4)]
    )
    blocks = [block] + [
        permuted(block, lambda x, q, z: at(x - shift, q, z)) for shift in range(1, NX)
    ]
    above, below = along_z(own, -1), along_z(own, 1)
    above, below, block = lax.optimization_barrier((above, below, block))
    planes = [own, above, below, along_z(above[:2], -1), along_z(below[:2], 1)]

    flops = 2 * 27 * GRID * FACE * size * out_size
    paired_shape = lambda deep, wide: shaped((2, 18 * deep, 2 * wide), bf16)
    columns_shape = shaped((GRID + 2, FACE + 2 * GRID, 3 * size), bf16)
    (columns,) = call(
        lambda where, *refs: store_columns(ring_pairs(where, Z_STEPS), refs[:-1], refs[-1]),
        where,
        planes,
        [columns_shape],
        [],
        0,
    )
    columns, blocks[1], blocks[3] = lax.optimization_barrier((columns, blocks[1], blocks[3]))
    ahead_weights, back_weights = call(
        weights_kernel,
        where,
        blocks,
        [paired_shape(size, out_size), paired_shape(out_size, size)],
        [pltpu.VMEM((27, size, out_size), bf16)],
        0,
    )
    def products(pairs, where, columns, weights, outs):
        return call(
            lambda *refs: product_kernel(pairs, *refs),
            where,
            [columns, weights],
            outs,
            [],
            flops // 2,
        )

    (send,) = products(other_pairs, where, columns, ahead_weights, [shaped((8, FACE, out_size), bf16)])
    where, send = lax.optimization_barrier((where, send))
    send = permuted(send, lambda x, q, z: at(x, q ^ 1, z)).astype(f32)
    keep = products(own_pairs, where, columns, ahead_weights, [shaped((2, FACE, out_size), f32)] * 4)
    keep = [piece + send[2 * r : 2 * r + 2] for r, piece in enumerate(keep)]
    pre_act = keep[0]
    for r in (2, 1, 3):
        pre_act = pre_act + permuted(
            keep[r].astype(bf16), lambda x, q, z: at(x, q + 2 * r, z)
        ).astype(f32)
    pre_act = pre_act + conv_bias[None, None, :]

    target = jnp.stack([cotangent[1], ahead])
    output, slope = gelu_pair(pre_act)
    activated = output.astype(bf16)
    grad_pre = (target.reshape(2, FACE, out_size).astype(f32) * slope).astype(bf16)

    slopes = [grad_pre]
    for r in range(1, 4):
        slopes.append(permuted(grad_pre, lambda x, q, z: at(x, q + 2 * r, z)))
    other = [permuted(piece, lambda x, q, z: at(x, q ^ 1, z)) for piece in slopes]
    slopes = slopes + other
    (slope_columns,) = call(slopes_kernel, where, slopes, [columns_shape], [], 0)

    scale = 1.0 / math.sqrt(NX * GRID * FACE)
    terms = call(
        lambda *refs: filters_kernel(scale, *refs),
        where,
        [columns] + slopes,
        [shaped((28, rows, out_size), bf16)] * NX,
        [
            pltpu.VMEM((out_size, (GRID + 2) * FACE), bf16),
            pltpu.VMEM((3 * out_size, 9 * size), f32),
            pltpu.VMEM((27, size, out_size), bf16),
        ],
        flops,
    )
    where, terms = lax.optimization_barrier((where, terms))
    def parts(steps, where, kinds):
        return call(
            lambda *refs: product_kernel(lambda where: ring_pairs(where, steps), *refs),
            where,
            [slope_columns, back_weights],
            [shaped((2, FACE, size), kind) for kind in kinds],
            [],
            flops * len(steps) // NZ,
        )

    up, down = parts((2, -2), where, [bf16, bf16])
    up, down, where = lax.optimization_barrier((up, down, where))
    up, down = along_z(up, 1).astype(f32), along_z(down, -1).astype(f32)
    above, far_above, below, far_below = parts((1, -3, -1, 3), where, [f32, bf16, f32, bf16])
    above, below, where = lax.optimization_barrier((above, below, where))
    above = jnp.concatenate([(above + up).astype(bf16), far_above])
    below = jnp.concatenate([(below + down).astype(bf16), far_below])
    above, below, where = lax.optimization_barrier((above, below, where))
    near, beyond = parts((0, 4), where, [f32, f32])
    near, beyond, terms = lax.optimization_barrier((near, beyond, terms))
    received = [
        permuted(terms[r], lambda x, q, z: at(x + r, q, z)) for r in range(1, NX)
    ]
    above, below = along_z(above, 1).astype(f32), along_z(below, -1).astype(f32)
    near = (near + above[:2] + below[:2]).astype(bf16)
    beyond = (beyond + above[2:] + below[2:]).astype(bf16)

    near, beyond, activated = lax.optimization_barrier((near, beyond, activated))

    def next_slab(plane):
        return permuted(plane, lambda x, q, z: device(NQ * x + q + 1, z))

    def home(step):
        return lambda x, q, z: device(NQ * x + (z - group(q) - step) % NZ, group(q))

    near, beyond = permuted(near, home(0)).astype(f32), permuted(beyond, home(4)).astype(f32)
    summed = (near + beyond).astype(bf16)
    shifted, received = lax.optimization_barrier((next_slab(activated[1]), received))
    held = sum((piece.astype(f32) for piece in received), terms[0].astype(f32))
    grad_bias = held[27, 0] + held[27, 1]
    grad_filters = permuted(
        held[:27].astype(bf16), lambda x, q, z: device(NX * group(q) + swapped(x), z)
    ).astype(f32)

    activated = jnp.stack([shifted, activated[0]])
    second, grad_filters = lax.optimization_barrier((next_slab(summed[1]), grad_filters))
    grad_input = jnp.stack([second, summed[0]])
    shape = (2, GRID, GRID)
    return (
        activated.reshape(*shape, out_size),
        grad_input.reshape(*shape, size),
        grad_filters.transpose(1, 0, 2),
        grad_bias,
    )


def solution(mesh):
    return jax.shard_map(
        on_device,
        mesh=mesh,
        in_specs=(
            P("space", None, None, "chan"),
            P("space", None, "chan"),
            P("chan"),
            P("space", None, None, "chan"),
        ),
        out_specs=(
            P("space", None, None, "chan"),
            P("space", None, None, "chan"),
            P("space", None, "chan"),
            P("chan"),
        ),
        check_vma=False,
    )
```

```python
import math

import jax
import jax.numpy as jnp
from jax import lax
from jax.experimental import pallas as pl
from jax.experimental.pallas import tpu as pltpu
from jax.sharding import PartitionSpec as P


GRID = 16
FACE = GRID * GRID
NX, NQ, NZ = 4, 8, 8
KAPPA = 0.7978845608028654
CUBIC = 0.044715
VMEM_LIMIT = 24 * 1024 * 1024
Z_STEPS = (0, 4, 1, -3, -1, 3, 2, -2)


def gelu_pair(values):
    inner = KAPPA * (values + CUBIC * values * values * values)
    tangent = jnp.tanh(inner)
    output = 0.5 * values * (1.0 + tangent)
    slope = 0.5 * (1.0 + tangent) + 0.5 * values * (1.0 - tangent * tangent) * KAPPA * (
        1.0 + 3.0 * CUBIC * values * values
    )
    return (output, slope)


def device(space, z):
    return space % (NX * NQ) * NZ + z % NZ


def at(x, q, z):
    return device(x % NX * NQ + q % NQ, z)


def permuted(array, target):
    pairs = [(at(x, q, z), target(x, q, z)) for x in range(NX) for q in range(NQ) for z in range(NZ)]
    return lax.ppermute(array, ("space", "chan"), pairs)


def group(q):
    return q // 2 + 4 * (q % 2)


def holder(group):
    return group % 4 * 2 + group // 4


def swapped(index):
    return index >> 1 | (index & 1) << 1


def position(where):
    space, z = where[0], where[1]
    q = space & (NQ - 1)
    return space >> 3, q, q >> 1, q & 1, z


def ring_pairs(where, steps):
    _, _, y, core, z = position(where)
    return [(z + r - y - 4 * core) & (NQ - 1) for r in steps]


def slope_pairs(where):
    _, _, y, core, _ = position(where)
    rows = [(y - r) & 3 for r in range(4)]
    return [2 * row + core for row in rows] + [2 * row + 1 - core for row in rows]


def store_columns(pairs, planes, columns):
    size = planes[0].shape[-1]
    width = lax.broadcasted_iota(jnp.int32, (FACE, size), 0) % GRID
    rows, whole = columns.shape[1:]
    columns[0] = jnp.zeros((rows, whole), jnp.bfloat16)
    columns[GRID + 1] = jnp.zeros((rows, whole), jnp.bfloat16)
    edge = jnp.zeros((GRID, whole), jnp.bfloat16)
    places = [(ref, 2 * index) for ref in planes for index in range(ref.shape[0] // 2)]
    for pair, (ref, start) in zip(pairs, places):
        for half in range(2):
            depth = 2 * pair + half + 1
            middle = ref[start + half]
            wide = middle.astype(jnp.float32)
            left = jnp.where(width == 0, 0.0, pltpu.roll(wide, 1, 0)).astype(jnp.bfloat16)
            right = jnp.where(width == GRID - 1, 0.0, pltpu.roll(wide, FACE - 1, 0)).astype(
                jnp.bfloat16
            )
            columns[depth, :GRID, :] = edge
            columns[depth, FACE + GRID :, :] = edge
            for c, value in enumerate((left, middle, right)):
                columns[depth, GRID : FACE + GRID, c * size : (c + 1) * size] = value


def window(columns, plane):
    return jnp.concatenate(
        [columns[plane, GRID * b : GRID * b + FACE, :] for b in range(3)], axis=1
    )


def convolved(columns, pairs, paired):
    left = jnp.concatenate(
        [
            jnp.concatenate([window(columns, 2 * pair + i) for i in range(4)], axis=1)
            for pair in pairs
        ],
        axis=0,
    )
    return jnp.dot(left, paired[...], preferred_element_type=jnp.float32)


def halves(product, index, size):
    rows = slice(index * FACE, (index + 1) * FACE)
    return [product[rows, o * size : (o + 1) * size] for o in range(2)]


def weights_kernel(turned, where, *refs):
    *blocks, paired, natural = refs
    rows = blocks[0].shape[1]
    x = position(where)[0]
    for r in range(NX):
        offset = pl.multiple_of(swapped((x + r) & (NX - 1)) * rows, rows)
        for tap in range(27):
            natural[tap, pl.ds(offset, rows)] = blocks[r][tap]
    deep, wide = natural.shape[1:][::-1] if turned else natural.shape[1:]
    none = jnp.zeros((9 * deep, wide), jnp.bfloat16)
    paired[: 9 * deep, wide:] = none
    paired[27 * deep :, :wide] = none
    for tap in range(27):
        block = natural[tap]
        if turned:
            block = block.T
        a, bc = (26 - tap) // 9 if turned else tap // 9, (26 - tap) % 9 if turned else tap % 9
        for o in range(2):
            first = ((a + o) * 9 + bc) * deep
            paired[first : first + deep, o * wide : (o + 1) * wide] = block


def own_pairs(where):
    _, _, y, core, _ = position(where)
    return [2 * ((y + r) & 3) + core for r in range(4)]


def other_pairs(where):
    _, _, y, core, _ = position(where)
    return [2 * ((y + r) & 3) + 1 - core for r in range(4)]


def slopes_kernel(where, *refs):
    store_columns(slope_pairs(where), refs[:NQ], refs[NQ])


def product_kernel(pairs, where, columns, paired, *outs):
    product = convolved(columns, pairs(where), paired)
    places = [(out, 2 * index) for out in outs for index in range(out.shape[0] // 2)]
    for index, (out, start) in enumerate(places):
        for half, value in enumerate(halves(product, index, out.shape[-1])):
            out[start + half] = value.astype(out.dtype)


def filters_kernel(scale, where, columns, *refs):
    planes, outs = refs[:NQ], refs[NQ : NQ + NX]
    turned, total, natural = refs[NQ + NX :]
    size, rows = natural.shape[-1], outs[0].shape[1]
    x = position(where)[0]
    turned[:, :FACE] = jnp.zeros((size, FACE), jnp.bfloat16)
    turned[:, (GRID + 1) * FACE :] = jnp.zeros((size, FACE), jnp.bfloat16)
    bias = jnp.zeros((8, size), jnp.float32)
    for pair, ref in zip(slope_pairs(where), planes):
        for half in range(2):
            value = ref[half].astype(jnp.float32)
            bias = bias + jnp.sum(value.reshape(FACE // 8, 8, size), axis=0)
            start = pl.multiple_of((2 * pair + half + 1) * FACE, FACE)
            turned[:, pl.ds(start, FACE)] = ref[half].T
    product = None
    for first in range(0, GRID, GRID // 2):
        left = jnp.concatenate(
            [turned[:, (first + 2 - a) * FACE : (first + 2 - a + GRID // 2) * FACE] for a in range(3)],
            axis=0,
        )
        right = jnp.concatenate(
            [window(columns, first + 1 + e) for e in range(GRID // 2)], axis=0
        )
        part = jnp.dot(left, right, preferred_element_type=jnp.float32)
        product = part if product is None else product + part
    total[...] = product
    for tap in range(27):
        a, bc = tap // 9, tap % 9
        block = total[a * size : (a + 1) * size, bc * size : (bc + 1) * size]
        natural[tap] = (block * scale).astype(jnp.bfloat16).T
    whole = jnp.sum(bias, axis=0, keepdims=True) * scale
    upper = whole.astype(jnp.bfloat16)
    lower = (whole - upper.astype(jnp.float32)).astype(jnp.bfloat16)
    row = lax.broadcasted_iota(jnp.int32, (rows, size), 0)
    spread = jnp.where(
        row == 0, upper.astype(jnp.float32), jnp.where(row == 1, lower.astype(jnp.float32), 0.0)
    )
    for r in range(NX):
        offset = pl.multiple_of(swapped((x + r) & (NX - 1)) * rows, rows)
        for tap in range(27):
            outs[r][tap] = natural[tap, pl.ds(offset, rows)]
        outs[r][27] = spread.astype(outs[r].dtype)


def call(kernel, where, operands, outs, scratch, flops):
    moved = sum(o.size * o.dtype.itemsize for o in operands)
    moved += sum(math.prod(o.shape) * o.dtype.itemsize for o in outs)
    vmem = pl.BlockSpec(memory_space=pltpu.VMEM)
    return pl.pallas_call(
        kernel,
        out_shape=outs,
        in_specs=[pl.BlockSpec(memory_space=pltpu.SMEM)] + [vmem] * len(operands),
        out_specs=[vmem] * len(outs),
        scratch_shapes=scratch,
        compiler_params=pltpu.CompilerParams(vmem_limit_bytes=VMEM_LIMIT),
        cost_estimate=pl.CostEstimate(flops=flops, bytes_accessed=moved, transcendentals=0),
    )(where, *operands)


def on_device(features, filters, conv_bias, cotangent):
    where = jnp.stack([lax.axis_index("space"), lax.axis_index("chan")]).astype(jnp.int32)
    size, rows = features.shape[-1], filters.shape[0]
    out_size = filters.shape[-1]
    bf16, f32 = jnp.bfloat16, jnp.float32
    shaped = jax.ShapeDtypeStruct

    def along_z(piece, r):
        return permuted(piece, lambda x, q, z: at(x, q, z + r))

    block = permuted(
        filters.transpose(1, 0, 2),
        lambda x, q, z: at(swapped(q % NX), holder((NQ * x + q) // NX), z),
    )
    seconds = permuted(
        jnp.stack([features[0], cotangent[0]]), lambda x, q, z: device(NQ * x + q - 1, z)
    )
    ahead = seconds[1]
    own = jnp.stack([features[1], seconds[0]]).reshape(2, FACE, size)
    own = jnp.concatenate(
        [permuted(own, lambda x, q, z: at(x, holder(z), z + q + step)) for step in (0, 4)]
    )
    blocks = [block] + [
        permuted(block, lambda x, q, z: at(x - shift, q, z)) for shift in range(1, NX)
    ]
    above, below = along_z(own, -1), along_z(own, 1)
    above, below, block = lax.optimization_barrier((above, below, block))
    planes = [own, above, below, along_z(above[:2], -1), along_z(below[:2], 1)]

    flops = 2 * 27 * GRID * FACE * size * out_size
    paired_shape = lambda deep, wide: shaped((36 * deep, 2 * wide), bf16)
    columns_shape = shaped((GRID + 2, FACE + 2 * GRID, 3 * size), bf16)
    (columns,) = call(
        lambda where, *refs: store_columns(ring_pairs(where, Z_STEPS), refs[:-1], refs[-1]),
        where,
        planes,
        [columns_shape],
        [],
        0,
    )
    columns, blocks[1], blocks[3] = lax.optimization_barrier((columns, blocks[1], blocks[3]))

    def weights(turned, where):
        (paired,) = call(
            lambda *refs: weights_kernel(turned, *refs),
            where,
            blocks,
            [paired_shape(out_size, size) if turned else paired_shape(size, out_size)],
            [pltpu.VMEM((27, size, out_size), bf16)],
            0,
        )
        return paired

    ahead_weights = weights(False, where)
    def products(pairs, where, columns, weights, outs):
        return call(
            lambda *refs: product_kernel(pairs, *refs),
            where,
            [columns, weights],
            outs,
            [],
            flops // 2,
        )

    (send,) = products(other_pairs, where, columns, ahead_weights, [shaped((8, FACE, out_size), bf16)])
    where, send = lax.optimization_barrier((where, send))
    send = permuted(send, lambda x, q, z: at(x, q ^ 1, z)).astype(f32)
    keep = products(own_pairs, where, columns, ahead_weights, [shaped((2, FACE, out_size), f32)] * 4)
    keep = [piece + send[2 * r : 2 * r + 2] for r, piece in enumerate(keep)]
    pre_act = keep[0]
    for r in (2, 1, 3):
        pre_act = pre_act + permuted(
            keep[r].astype(bf16), lambda x, q, z: at(x, q + 2 * r, z)
        ).astype(f32)
    back_weights = weights(True, where)
    pre_act, back_weights = lax.optimization_barrier((pre_act, back_weights))
    pre_act = pre_act + conv_bias[None, None, :]

    target = jnp.stack([cotangent[1], ahead])
    output, slope = gelu_pair(pre_act)
    activated = output.astype(bf16)
    grad_pre = (target.reshape(2, FACE, out_size).astype(f32) * slope).astype(bf16)

    slopes = [grad_pre]
    for r in range(1, 4):
        slopes.append(permuted(grad_pre, lambda x, q, z: at(x, q + 2 * r, z)))
    other = [permuted(piece, lambda x, q, z: at(x, q ^ 1, z)) for piece in slopes]
    slopes = slopes + other
    (slope_columns,) = call(slopes_kernel, where, slopes, [columns_shape], [], 0)

    scale = 1.0 / math.sqrt(NX * GRID * FACE)
    terms = call(
        lambda *refs: filters_kernel(scale, *refs),
        where,
        [columns] + slopes,
        [shaped((28, rows, out_size), bf16)] * NX,
        [
            pltpu.VMEM((out_size, (GRID + 2) * FACE), bf16),
            pltpu.VMEM((3 * out_size, 9 * size), f32),
            pltpu.VMEM((27, size, out_size), bf16),
        ],
        flops,
    )
    where, terms = lax.optimization_barrier((where, terms))
    def parts(steps, where, kinds):
        return call(
            lambda *refs: product_kernel(lambda where: ring_pairs(where, steps), *refs),
            where,
            [slope_columns, back_weights],
            [shaped((2, FACE, size), kind) for kind in kinds],
            [],
            flops * len(steps) // NZ,
        )

    up, down = parts((2, -2), where, [bf16, bf16])
    up, down, where = lax.optimization_barrier((up, down, where))
    up, down = along_z(up, 1).astype(f32), along_z(down, -1).astype(f32)
    above, far_above, below, far_below = parts((1, -3, -1, 3), where, [f32, bf16, f32, bf16])
    above, below, where = lax.optimization_barrier((above, below, where))
    above = jnp.concatenate([(above + up).astype(bf16), far_above])
    below = jnp.concatenate([(below + down).astype(bf16), far_below])
    above, below, where = lax.optimization_barrier((above, below, where))
    near, beyond = parts((0, 4), where, [f32, f32])
    near, beyond, terms = lax.optimization_barrier((near, beyond, terms))
    received = [
        permuted(terms[r], lambda x, q, z: at(x + r, q, z)) for r in range(1, NX)
    ]
    above, below = along_z(above, 1).astype(f32), along_z(below, -1).astype(f32)
    near = (near + above[:2] + below[:2]).astype(bf16)
    beyond = (beyond + above[2:] + below[2:]).astype(bf16)

    near, beyond, activated = lax.optimization_barrier((near, beyond, activated))

    def next_slab(plane):
        return permuted(plane, lambda x, q, z: device(NQ * x + q + 1, z))

    def home(step):
        return lambda x, q, z: device(NQ * x + (z - group(q) - step) % NZ, group(q))

    near, beyond = permuted(near, home(0)).astype(f32), permuted(beyond, home(4)).astype(f32)
    summed = (near + beyond).astype(bf16)
    shifted, received = lax.optimization_barrier((next_slab(activated[1]), received))
    held = sum((piece.astype(f32) for piece in received), terms[0].astype(f32))
    grad_bias = held[27, 0] + held[27, 1]
    grad_filters = permuted(
        held[:27].astype(bf16), lambda x, q, z: device(NX * group(q) + swapped(x), z)
    ).astype(f32)

    activated = jnp.stack([shifted, activated[0]])
    second, grad_filters = lax.optimization_barrier((next_slab(summed[1]), grad_filters))
    grad_input = jnp.stack([second, summed[0]])
    shape = (2, GRID, GRID)
    return (
        activated.reshape(*shape, out_size),
        grad_input.reshape(*shape, size),
        grad_filters.transpose(1, 0, 2),
        grad_bias,
    )


def solution(mesh):
    return jax.shard_map(
        on_device,
        mesh=mesh,
        in_specs=(
            P("space", None, None, "chan"),
            P("space", None, "chan"),
            P("chan"),
            P("space", None, None, "chan"),
        ),
        out_specs=(
            P("space", None, None, "chan"),
            P("space", None, None, "chan"),
            P("space", None, "chan"),
            P("chan"),
        ),
        check_vma=False,
    )
```

```python
import math

import jax
import jax.numpy as jnp
from jax import lax
from jax.experimental import pallas as pl
from jax.experimental.pallas import tpu as pltpu
from jax.sharding import PartitionSpec as P


GRID = 16
FACE = GRID * GRID
NX, NQ, NZ = 4, 8, 8
KAPPA = 0.7978845608028654
CUBIC = 0.044715
VMEM_LIMIT = 24 * 1024 * 1024
Z_STEPS = (0, 4, 1, -3, -1, 3, 2, -2)


def gelu_pair(values):
    inner = KAPPA * (values + CUBIC * values * values * values)
    tangent = jnp.tanh(inner)
    output = 0.5 * values * (1.0 + tangent)
    slope = 0.5 * (1.0 + tangent) + 0.5 * values * (1.0 - tangent * tangent) * KAPPA * (
        1.0 + 3.0 * CUBIC * values * values
    )
    return (output, slope)


def device(space, z):
    return space % (NX * NQ) * NZ + z % NZ


def at(x, q, z):
    return device(x % NX * NQ + q % NQ, z)


def permuted(array, target):
    pairs = [(at(x, q, z), target(x, q, z)) for x in range(NX) for q in range(NQ) for z in range(NZ)]
    return lax.ppermute(array, ("space", "chan"), pairs)


def group(q):
    return q // 2 + 4 * (q % 2)


def holder(group):
    return group % 4 * 2 + group // 4


def swapped(index):
    return index >> 1 | (index & 1) << 1


def position(where):
    space, z = where[0], where[1]
    q = space & (NQ - 1)
    return space >> 3, q, q >> 1, q & 1, z


def ring_pairs(where, steps):
    _, _, y, core, z = position(where)
    return [(z + r - y - 4 * core) & (NQ - 1) for r in steps]


def slope_pairs(where):
    _, _, y, core, _ = position(where)
    rows = [(y - r) & 3 for r in range(4)]
    return [2 * row + core for row in rows] + [2 * row + 1 - core for row in rows]


def store_columns(pairs, planes, columns):
    size = planes[0].shape[-1]
    width = lax.broadcasted_iota(jnp.int32, (FACE, size), 0) % GRID
    rows, whole = columns.shape[1:]
    columns[0] = jnp.zeros((rows, whole), jnp.bfloat16)
    columns[GRID + 1] = jnp.zeros((rows, whole), jnp.bfloat16)
    edge = jnp.zeros((GRID, whole), jnp.bfloat16)
    places = [(ref, 2 * index) for ref in planes for index in range(ref.shape[0] // 2)]
    for pair, (ref, start) in zip(pairs, places):
        for half in range(2):
            depth = 2 * pair + half + 1
            middle = ref[start + half]
            wide = middle.astype(jnp.float32)
            left = jnp.where(width == 0, 0.0, pltpu.roll(wide, 1, 0)).astype(jnp.bfloat16)
            right = jnp.where(width == GRID - 1, 0.0, pltpu.roll(wide, FACE - 1, 0)).astype(
                jnp.bfloat16
            )
            columns[depth, :GRID, :] = edge
            columns[depth, FACE + GRID :, :] = edge
            for c, value in enumerate((left, middle, right)):
                columns[depth, GRID : FACE + GRID, c * size : (c + 1) * size] = value


def window(columns, plane):
    return jnp.concatenate(
        [columns[plane, GRID * b : GRID * b + FACE, :] for b in range(3)], axis=1
    )


def convolved(columns, pairs, paired):
    left = jnp.concatenate(
        [
            jnp.concatenate([window(columns, 2 * pair + i) for i in range(4)], axis=1)
            for pair in pairs
        ],
        axis=0,
    )
    return jnp.dot(left, paired[...], preferred_element_type=jnp.float32)


def halves(product, index, size):
    rows = slice(index * FACE, (index + 1) * FACE)
    return [product[rows, o * size : (o + 1) * size] for o in range(2)]


def weights_kernel(turned, where, *refs):
    *blocks, paired, natural = refs
    rows = blocks[0].shape[1]
    x = position(where)[0]
    for r in range(NX):
        offset = pl.multiple_of(swapped((x + r) & (NX - 1)) * rows, rows)
        for tap in range(27):
            natural[tap, pl.ds(offset, rows)] = blocks[r][tap]
    deep, wide = natural.shape[1:][::-1] if turned else natural.shape[1:]
    none = jnp.zeros((9 * deep, wide), jnp.bfloat16)
    paired[: 9 * deep, wide:] = none
    paired[27 * deep :, :wide] = none
    for tap in range(27):
        block = natural[tap]
        if turned:
            block = block.T
        a, bc = (26 - tap) // 9 if turned else tap // 9, (26 - tap) % 9 if turned else tap % 9
        for o in range(2):
            first = ((a + o) * 9 + bc) * deep
            paired[first : first + deep, o * wide : (o + 1) * wide] = block


def own_pairs(where):
    _, _, y, core, _ = position(where)
    return [2 * ((y + r) & 3) + core for r in range(4)]


def other_pairs(where):
    _, _, y, core, _ = position(where)
    return [2 * ((y + r) & 3) + 1 - core for r in range(4)]


def slopes_kernel(where, *refs):
    store_columns(slope_pairs(where), refs[:NQ], refs[NQ])


def product_kernel(pairs, where, columns, paired, *outs):
    product = convolved(columns, pairs(where), paired)
    places = [(out, 2 * index) for out in outs for index in range(out.shape[0] // 2)]
    for index, (out, start) in enumerate(places):
        for half, value in enumerate(halves(product, index, out.shape[-1])):
            out[start + half] = value.astype(out.dtype)


def filters_kernel(scale, where, columns, *refs):
    planes, outs = refs[:NQ], refs[NQ : NQ + NX]
    turned, total, natural = refs[NQ + NX :]
    size, rows = natural.shape[-1], outs[0].shape[1]
    x = position(where)[0]
    turned[:, :FACE] = jnp.zeros((size, FACE), jnp.bfloat16)
    turned[:, (GRID + 1) * FACE :] = jnp.zeros((size, FACE), jnp.bfloat16)
    bias = jnp.zeros((8, size), jnp.float32)
    for pair, ref in zip(slope_pairs(where), planes):
        for half in range(2):
            value = ref[half].astype(jnp.float32)
            bias = bias + jnp.sum(value.reshape(FACE // 8, 8, size), axis=0)
            start = pl.multiple_of((2 * pair + half + 1) * FACE, FACE)
            turned[:, pl.ds(start, FACE)] = ref[half].T
    product = None
    for first in range(0, GRID, GRID // 2):
        left = jnp.concatenate(
            [turned[:, (first + 2 - a) * FACE : (first + 2 - a + GRID // 2) * FACE] for a in range(3)],
            axis=0,
        )
        right = jnp.concatenate(
            [window(columns, first + 1 + e) for e in range(GRID // 2)], axis=0
        )
        part = jnp.dot(left, right, preferred_element_type=jnp.float32)
        product = part if product is None else product + part
    total[...] = product
    for tap in range(27):
        a, bc = tap // 9, tap % 9
        block = total[a * size : (a + 1) * size, bc * size : (bc + 1) * size]
        natural[tap] = (block * scale).astype(jnp.bfloat16).T
    whole = jnp.sum(bias, axis=0, keepdims=True) * scale
    upper = whole.astype(jnp.bfloat16)
    lower = (whole - upper.astype(jnp.float32)).astype(jnp.bfloat16)
    row = lax.broadcasted_iota(jnp.int32, (rows, size), 0)
    spread = jnp.where(
        row == 0, upper.astype(jnp.float32), jnp.where(row == 1, lower.astype(jnp.float32), 0.0)
    )
    for r in range(NX):
        offset = pl.multiple_of(swapped((x + r) & (NX - 1)) * rows, rows)
        for tap in range(27):
            outs[r][tap] = natural[tap, pl.ds(offset, rows)]
        outs[r][27] = spread.astype(outs[r].dtype)


def call(kernel, where, operands, outs, scratch, flops):
    moved = sum(o.size * o.dtype.itemsize for o in operands)
    moved += sum(math.prod(o.shape) * o.dtype.itemsize for o in outs)
    vmem = pl.BlockSpec(memory_space=pltpu.VMEM)
    return pl.pallas_call(
        kernel,
        out_shape=outs,
        in_specs=[pl.BlockSpec(memory_space=pltpu.SMEM)] + [vmem] * len(operands),
        out_specs=[vmem] * len(outs),
        scratch_shapes=scratch,
        compiler_params=pltpu.CompilerParams(vmem_limit_bytes=VMEM_LIMIT),
        cost_estimate=pl.CostEstimate(flops=flops, bytes_accessed=moved, transcendentals=0),
    )(where, *operands)


def on_device(features, filters, conv_bias, cotangent):
    where = jnp.stack([lax.axis_index("space"), lax.axis_index("chan")]).astype(jnp.int32)
    size, rows = features.shape[-1], filters.shape[0]
    out_size = filters.shape[-1]
    bf16, f32 = jnp.bfloat16, jnp.float32
    shaped = jax.ShapeDtypeStruct

    def along_z(piece, r):
        return permuted(piece, lambda x, q, z: at(x, q, z + r))

    block = permuted(
        filters.transpose(1, 0, 2),
        lambda x, q, z: at(swapped(q % NX), holder((NQ * x + q) // NX), z),
    )
    seconds = permuted(
        jnp.stack([features[0], cotangent[0]]), lambda x, q, z: device(NQ * x + q - 1, z)
    )
    ahead = seconds[1]
    own = jnp.stack([features[1], seconds[0]]).reshape(2, FACE, size)
    own = jnp.concatenate(
        [permuted(own, lambda x, q, z: at(x, holder(z), z + q + step)) for step in (0, 4)]
    )
    blocks = [block] + [
        permuted(block, lambda x, q, z: at(x - shift, q, z)) for shift in range(1, NX)
    ]
    above, below = along_z(own, -1), along_z(own, 1)
    above, below, block = lax.optimization_barrier((above, below, block))
    planes = [own, above, below, along_z(above[:2], -1), along_z(below[:2], 1)]

    flops = 2 * 27 * GRID * FACE * size * out_size
    paired_shape = lambda deep, wide: shaped((36 * deep, 2 * wide), bf16)
    columns_shape = shaped((GRID + 2, FACE + 2 * GRID, 3 * size), bf16)
    (columns,) = call(
        lambda where, *refs: store_columns(ring_pairs(where, Z_STEPS), refs[:-1], refs[-1]),
        where,
        planes,
        [columns_shape],
        [],
        0,
    )
    columns, blocks[1], blocks[3] = lax.optimization_barrier((columns, blocks[1], blocks[3]))

    def weights(turned, where):
        (paired,) = call(
            lambda *refs: weights_kernel(turned, *refs),
            where,
            blocks,
            [paired_shape(out_size, size) if turned else paired_shape(size, out_size)],
            [pltpu.VMEM((27, size, out_size), bf16)],
            0,
        )
        return paired

    ahead_weights = weights(False, where)
    def products(pairs, where, columns, weights, outs):
        return call(
            lambda *refs: product_kernel(pairs, *refs),
            where,
            [columns, weights],
            outs,
            [],
            flops // 2,
        )

    (send,) = products(other_pairs, where, columns, ahead_weights, [shaped((8, FACE, out_size), bf16)])
    where, send = lax.optimization_barrier((where, send))
    send = permuted(send, lambda x, q, z: at(x, q ^ 1, z)).astype(f32)
    keep = products(own_pairs, where, columns, ahead_weights, [shaped((2, FACE, out_size), f32)] * 4)
    keep = [piece + send[2 * r : 2 * r + 2] for r, piece in enumerate(keep)]
    pre_act = keep[0]
    for r in (2, 1, 3):
        pre_act = pre_act + permuted(
            keep[r].astype(bf16), lambda x, q, z: at(x, q + 2 * r, z)
        ).astype(f32)
    back_weights = weights(True, where)
    pre_act, back_weights = lax.optimization_barrier((pre_act, back_weights))
    pre_act = pre_act + conv_bias[None, None, :]

    target = jnp.stack([cotangent[1], ahead])
    output, slope = gelu_pair(pre_act)
    activated = output.astype(bf16)
    grad_pre = (target.reshape(2, FACE, out_size).astype(f32) * slope).astype(bf16)

    slopes = [grad_pre]
    for r in range(1, 4):
        slopes.append(permuted(grad_pre, lambda x, q, z: at(x, q + 2 * r, z)))
    other = [permuted(piece, lambda x, q, z: at(x, q ^ 1, z)) for piece in slopes]
    slopes = slopes + other
    (slope_columns,) = call(slopes_kernel, where, slopes, [columns_shape], [], 0)

    scale = 1.0 / math.sqrt(NX * GRID * FACE)
    terms = call(
        lambda *refs: filters_kernel(scale, *refs),
        where,
        [columns] + slopes,
        [shaped((28, rows, out_size), bf16)] * NX,
        [
            pltpu.VMEM((out_size, (GRID + 2) * FACE), bf16),
            pltpu.VMEM((3 * out_size, 9 * size), f32),
            pltpu.VMEM((27, size, out_size), bf16),
        ],
        flops,
    )
    where, terms = lax.optimization_barrier((where, terms))
    def parts(steps, where, outs):
        return call(
            lambda *refs: product_kernel(lambda where: ring_pairs(where, steps), *refs),
            where,
            [slope_columns, back_weights],
            outs,
            [],
            flops * len(steps) // NZ,
        )

    received = [permuted(terms[2], lambda x, q, z: at(x + 2, q, z))]
    up, down = parts((2, -3, -2, 3), where, [shaped((4, FACE, size), bf16)] * 2)
    up, down, where = lax.optimization_barrier((up, down, where))
    up, down = along_z(up, 1), along_z(down, -1)
    above, below, beyond, summed = parts((1, -1, 4, 0), where, [shaped((2, FACE, size), f32)] * 4)
    above, below, beyond, summed, *later = lax.optimization_barrier(
        (above, below, beyond, summed, terms[1], terms[3])
    )
    received.append(permuted(later[0], lambda x, q, z: at(x + 1, q, z)))
    received.append(permuted(later[1], lambda x, q, z: at(x + 3, q, z)))
    above = (above + up[:2].astype(f32)).astype(bf16)
    below = (below + down[:2].astype(f32)).astype(bf16)
    beyond = (beyond + up[2:].astype(f32) + down[2:].astype(f32)).astype(bf16)
    beyond, above, below = along_z(beyond, 4), along_z(above, 1), along_z(below, -1)
    held = sum((piece.astype(f32) for piece in received), terms[0].astype(f32))
    grad_bias = held[27, 0] + held[27, 1]
    grad_filters = permuted(
        held[:27].astype(bf16), lambda x, q, z: device(NX * group(q) + swapped(x), z)
    ).astype(f32)
    summed = summed + beyond.astype(f32) + above.astype(f32) + below.astype(f32)
    summed, activated = lax.optimization_barrier((summed.astype(bf16), activated))

    def home(half):
        return lambda x, q, z: device(NQ * x + (z - group(q)) % NZ + half, group(q))

    first, second = permuted(summed[0], home(0)), permuted(summed[1], home(1))
    shifted = permuted(activated[1], lambda x, q, z: device(NQ * x + q + 1, z))
    activated = jnp.stack([shifted, activated[0]])
    second, grad_filters = lax.optimization_barrier((second, grad_filters))
    grad_input = jnp.stack([second, first])
    shape = (2, GRID, GRID)
    return (
        activated.reshape(*shape, out_size),
        grad_input.reshape(*shape, size),
        grad_filters.transpose(1, 0, 2),
        grad_bias,
    )


def solution(mesh):
    return jax.shard_map(
        on_device,
        mesh=mesh,
        in_specs=(
            P("space", None, None, "chan"),
            P("space", None, "chan"),
            P("chan"),
            P("space", None, None, "chan"),
        ),
        out_specs=(
            P("space", None, None, "chan"),
            P("space", None, None, "chan"),
            P("space", None, "chan"),
            P("chan"),
        ),
        check_vma=False,
    )
```

```python
import math

import jax
import jax.numpy as jnp
from jax import lax
from jax.experimental import pallas as pl
from jax.experimental.pallas import tpu as pltpu
from jax.sharding import PartitionSpec as P


GRID = 16
FACE = GRID * GRID
NX, NQ, NZ = 4, 8, 8
KAPPA = 0.7978845608028654
CUBIC = 0.044715
VMEM_LIMIT = 24 * 1024 * 1024
Z_STEPS = (0, 4, 1, -3, -1, 3, 2, -2)


def gelu_pair(values):
    inner = KAPPA * (values + CUBIC * values * values * values)
    tangent = jnp.tanh(inner)
    output = 0.5 * values * (1.0 + tangent)
    slope = 0.5 * (1.0 + tangent) + 0.5 * values * (1.0 - tangent * tangent) * KAPPA * (
        1.0 + 3.0 * CUBIC * values * values
    )
    return (output, slope)


def device(space, z):
    return space % (NX * NQ) * NZ + z % NZ


def at(x, q, z):
    return device(x % NX * NQ + q % NQ, z)


def permuted(array, target):
    pairs = [(at(x, q, z), target(x, q, z)) for x in range(NX) for q in range(NQ) for z in range(NZ)]
    return lax.ppermute(array, ("space", "chan"), pairs)


def group(q):
    return q // 2 + 4 * (q % 2)


def holder(group):
    return group % 4 * 2 + group // 4


def swapped(index):
    return index >> 1 | (index & 1) << 1


def position(where):
    space, z = where[0], where[1]
    q = space & (NQ - 1)
    return space >> 3, q, q >> 1, q & 1, z


def ring_pairs(where, steps):
    _, _, y, core, z = position(where)
    return [(z + r - y - 4 * core) & (NQ - 1) for r in steps]


def slope_pairs(where):
    _, _, y, core, _ = position(where)
    rows = [(y - r) & 3 for r in range(4)]
    return [2 * row + core for row in rows] + [2 * row + 1 - core for row in rows]


def store_columns(pairs, planes, columns):
    size = planes[0].shape[-1]
    width = lax.broadcasted_iota(jnp.int32, (FACE, size), 0) % GRID
    rows, whole = columns.shape[1:]
    columns[0] = jnp.zeros((rows, whole), jnp.bfloat16)
    columns[GRID + 1] = jnp.zeros((rows, whole), jnp.bfloat16)
    edge = jnp.zeros((GRID, whole), jnp.bfloat16)
    places = [(ref, 2 * index) for ref in planes for index in range(ref.shape[0] // 2)]
    for pair, (ref, start) in zip(pairs, places):
        for half in range(2):
            depth = 2 * pair + half + 1
            middle = ref[start + half]
            wide = middle.astype(jnp.float32)
            left = jnp.where(width == 0, 0.0, pltpu.roll(wide, 1, 0)).astype(jnp.bfloat16)
            right = jnp.where(width == GRID - 1, 0.0, pltpu.roll(wide, FACE - 1, 0)).astype(
                jnp.bfloat16
            )
            columns[depth, :GRID, :] = edge
            columns[depth, FACE + GRID :, :] = edge
            for c, value in enumerate((left, middle, right)):
                columns[depth, GRID : FACE + GRID, c * size : (c + 1) * size] = value


def window(columns, plane):
    return jnp.concatenate(
        [columns[plane, GRID * b : GRID * b + FACE, :] for b in range(3)], axis=1
    )


def convolved(columns, pairs, paired):
    left = jnp.concatenate(
        [
            jnp.concatenate([window(columns, 2 * pair + i) for i in range(4)], axis=1)
            for pair in pairs
        ],
        axis=0,
    )
    return jnp.dot(left, paired[...], preferred_element_type=jnp.float32)


def halves(product, index, size):
    rows = slice(index * FACE, (index + 1) * FACE)
    return [product[rows, o * size : (o + 1) * size] for o in range(2)]


def weights_kernel(turned, where, *refs):
    *blocks, paired, natural = refs
    rows = blocks[0].shape[1]
    x = position(where)[0]
    for r in range(NX):
        offset = pl.multiple_of(swapped((x + r) & (NX - 1)) * rows, rows)
        for tap in range(27):
            natural[tap, pl.ds(offset, rows)] = blocks[r][tap]
    deep, wide = natural.shape[1:][::-1] if turned else natural.shape[1:]
    none = jnp.zeros((9 * deep, wide), jnp.bfloat16)
    paired[: 9 * deep, wide:] = none
    paired[27 * deep :, :wide] = none
    for tap in range(27):
        block = natural[tap]
        if turned:
            block = block.T
        a, bc = (26 - tap) // 9 if turned else tap // 9, (26 - tap) % 9 if turned else tap % 9
        for o in range(2):
            first = ((a + o) * 9 + bc) * deep
            paired[first : first + deep, o * wide : (o + 1) * wide] = block


def own_pairs(where):
    _, _, y, core, _ = position(where)
    return [2 * ((y + r) & 3) + core for r in range(4)]


def other_pairs(where):
    _, _, y, core, _ = position(where)
    return [2 * ((y + r) & 3) + 1 - core for r in range(4)]


def slopes_kernel(where, *refs):
    store_columns(slope_pairs(where), refs[:NQ], refs[NQ])


def product_kernel(pairs, where, columns, paired, *outs):
    product = convolved(columns, pairs(where), paired)
    places = [(out, 2 * index) for out in outs for index in range(out.shape[0] // 2)]
    for index, (out, start) in enumerate(places):
        for half, value in enumerate(halves(product, index, out.shape[-1])):
            out[start + half] = value.astype(out.dtype)


def filters_kernel(scale, where, columns, *refs):
    planes, outs = refs[:NQ], refs[NQ : NQ + NX]
    turned, total, natural = refs[NQ + NX :]
    size, rows = natural.shape[-1], outs[0].shape[1]
    x = position(where)[0]
    turned[:, :FACE] = jnp.zeros((size, FACE), jnp.bfloat16)
    turned[:, (GRID + 1) * FACE :] = jnp.zeros((size, FACE), jnp.bfloat16)
    bias = jnp.zeros((8, size), jnp.float32)
    for pair, ref in zip(slope_pairs(where), planes):
        for half in range(2):
            value = ref[half].astype(jnp.float32)
            bias = bias + jnp.sum(value.reshape(FACE // 8, 8, size), axis=0)
            start = pl.multiple_of((2 * pair + half + 1) * FACE, FACE)
            turned[:, pl.ds(start, FACE)] = ref[half].T
    product = None
    for first in range(0, GRID, GRID // 2):
        left = jnp.concatenate(
            [turned[:, (first + 2 - a) * FACE : (first + 2 - a + GRID // 2) * FACE] for a in range(3)],
            axis=0,
        )
        right = jnp.concatenate(
            [window(columns, first + 1 + e) for e in range(GRID // 2)], axis=0
        )
        part = jnp.dot(left, right, preferred_element_type=jnp.float32)
        product = part if product is None else product + part
    total[...] = product
    for tap in range(27):
        a, bc = tap // 9, tap % 9
        block = total[a * size : (a + 1) * size, bc * size : (bc + 1) * size]
        natural[tap] = (block * scale).astype(jnp.bfloat16).T
    whole = jnp.sum(bias, axis=0, keepdims=True) * scale
    upper = whole.astype(jnp.bfloat16)
    lower = (whole - upper.astype(jnp.float32)).astype(jnp.bfloat16)
    row = lax.broadcasted_iota(jnp.int32, (rows, size), 0)
    spread = jnp.where(
        row == 0, upper.astype(jnp.float32), jnp.where(row == 1, lower.astype(jnp.float32), 0.0)
    )
    for r in range(NX):
        offset = pl.multiple_of(swapped((x + r) & (NX - 1)) * rows, rows)
        for tap in range(27):
            outs[r][tap] = natural[tap, pl.ds(offset, rows)]
        outs[r][27] = spread.astype(outs[r].dtype)


def call(kernel, where, operands, outs, scratch, flops):
    moved = sum(o.size * o.dtype.itemsize for o in operands)
    moved += sum(math.prod(o.shape) * o.dtype.itemsize for o in outs)
    vmem = pl.BlockSpec(memory_space=pltpu.VMEM)
    return pl.pallas_call(
        kernel,
        out_shape=outs,
        in_specs=[pl.BlockSpec(memory_space=pltpu.SMEM)] + [vmem] * len(operands),
        out_specs=[vmem] * len(outs),
        scratch_shapes=scratch,
        compiler_params=pltpu.CompilerParams(vmem_limit_bytes=VMEM_LIMIT),
        cost_estimate=pl.CostEstimate(flops=flops, bytes_accessed=moved, transcendentals=0),
    )(where, *operands)


def on_device(features, filters, conv_bias, cotangent):
    where = jnp.stack([lax.axis_index("space"), lax.axis_index("chan")]).astype(jnp.int32)
    size, rows = features.shape[-1], filters.shape[0]
    out_size = filters.shape[-1]
    bf16, f32 = jnp.bfloat16, jnp.float32
    shaped = jax.ShapeDtypeStruct

    def along_z(piece, r):
        return permuted(piece, lambda x, q, z: at(x, q, z + r))

    block = permuted(
        filters.transpose(1, 0, 2),
        lambda x, q, z: at(swapped(q % NX), holder((NQ * x + q) // NX), z),
    )
    seconds = permuted(
        jnp.stack([features[0], cotangent[0]]), lambda x, q, z: device(NQ * x + q - 1, z)
    )
    ahead = seconds[1]
    own = jnp.stack([features[1], seconds[0]]).reshape(2, FACE, size)
    own = jnp.concatenate(
        [permuted(own, lambda x, q, z: at(x, holder(z), z + q + step)) for step in (0, 4)]
    )
    blocks = [block] * NX
    for shift in (2, 1, 3):
        blocks[shift] = permuted(block, lambda x, q, z: at(x - shift, q, z))
    above, below = along_z(own, -1), along_z(own, 1)
    above, below, block = lax.optimization_barrier((above, below, block))
    planes = [own, above, below, along_z(above[:2], -1), along_z(below[:2], 1)]

    flops = 2 * 27 * GRID * FACE * size * out_size
    paired_shape = lambda deep, wide: shaped((36 * deep, 2 * wide), bf16)
    columns_shape = shaped((GRID + 2, FACE + 2 * GRID, 3 * size), bf16)
    (columns,) = call(
        lambda where, *refs: store_columns(ring_pairs(where, Z_STEPS), refs[:-1], refs[-1]),
        where,
        planes,
        [columns_shape],
        [],
        0,
    )
    columns, blocks[2] = lax.optimization_barrier((columns, blocks[2]))

    def weights(turned, where):
        (paired,) = call(
            lambda *refs: weights_kernel(turned, *refs),
            where,
            blocks,
            [paired_shape(out_size, size) if turned else paired_shape(size, out_size)],
            [pltpu.VMEM((27, size, out_size), bf16)],
            0,
        )
        return paired

    ahead_weights = weights(False, where)
    def products(pairs, where, columns, weights, outs):
        return call(
            lambda *refs: product_kernel(pairs, *refs),
            where,
            [columns, weights],
            outs,
            [],
            flops // 2,
        )

    (send,) = products(other_pairs, where, columns, ahead_weights, [shaped((8, FACE, out_size), bf16)])
    where, send = lax.optimization_barrier((where, send))
    send = permuted(send, lambda x, q, z: at(x, q ^ 1, z)).astype(f32)
    keep = products(own_pairs, where, columns, ahead_weights, [shaped((2, FACE, out_size), f32)] * 4)
    keep = [piece + send[2 * r : 2 * r + 2] for r, piece in enumerate(keep)]
    pre_act = keep[0]
    for r in (2, 1, 3):
        pre_act = pre_act + permuted(
            keep[r].astype(bf16), lambda x, q, z: at(x, q + 2 * r, z)
        ).astype(f32)
    back_weights = weights(True, where)
    pre_act, back_weights = lax.optimization_barrier((pre_act, back_weights))
    pre_act = pre_act + conv_bias[None, None, :]

    target = jnp.stack([cotangent[1], ahead])
    output, slope = gelu_pair(pre_act)
    activated = output.astype(bf16)
    grad_pre = (target.reshape(2, FACE, out_size).astype(f32) * slope).astype(bf16)

    slopes = [grad_pre]
    for r in range(1, 4):
        slopes.append(permuted(grad_pre, lambda x, q, z: at(x, q + 2 * r, z)))
    other = [permuted(piece, lambda x, q, z: at(x, q ^ 1, z)) for piece in slopes]
    slopes = slopes + other
    (slope_columns,) = call(slopes_kernel, where, slopes, [columns_shape], [], 0)

    scale = 1.0 / math.sqrt(NX * GRID * FACE)
    terms = call(
        lambda *refs: filters_kernel(scale, *refs),
        where,
        [columns] + slopes,
        [shaped((28, rows, out_size), bf16)] * NX,
        [
            pltpu.VMEM((out_size, (GRID + 2) * FACE), bf16),
            pltpu.VMEM((3 * out_size, 9 * size), f32),
            pltpu.VMEM((27, size, out_size), bf16),
        ],
        flops,
    )
    where, terms = lax.optimization_barrier((where, terms))
    def parts(steps, where, outs):
        return call(
            lambda *refs: product_kernel(lambda where: ring_pairs(where, steps), *refs),
            where,
            [slope_columns, back_weights],
            outs,
            [],
            flops * len(steps) // NZ,
        )

    received = [permuted(terms[2], lambda x, q, z: at(x + 2, q, z))]
    up, down = parts((2, -3, -2, 3), where, [shaped((4, FACE, size), bf16)] * 2)
    up, down, where = lax.optimization_barrier((up, down, where))
    up, down = along_z(up, 1), along_z(down, -1)
    above, below, beyond, summed = parts((1, -1, 4, 0), where, [shaped((2, FACE, size), f32)] * 4)
    above, below, beyond, summed, *later = lax.optimization_barrier(
        (above, below, beyond, summed, terms[1], terms[3])
    )
    received.append(permuted(later[0], lambda x, q, z: at(x + 1, q, z)))
    received.append(permuted(later[1], lambda x, q, z: at(x + 3, q, z)))
    above = (above + up[:2].astype(f32)).astype(bf16)
    below = (below + down[:2].astype(f32)).astype(bf16)
    beyond = (beyond + up[2:].astype(f32) + down[2:].astype(f32)).astype(bf16)
    beyond, above, below = along_z(beyond, 4), along_z(above, 1), along_z(below, -1)
    held = sum((piece.astype(f32) for piece in received), terms[0].astype(f32))
    bias_rows = held[27, :2]
    grad_filters = permuted(
        held[:27].astype(bf16), lambda x, q, z: device(NX * group(q) + swapped(x), z)
    ).astype(f32)
    summed = summed + beyond.astype(f32) + above.astype(f32) + below.astype(f32)
    summed, activated = lax.optimization_barrier((summed.astype(bf16), activated))

    def home(half):
        return lambda x, q, z: device(NQ * x + (z - group(q)) % NZ + half, group(q))

    first, second = permuted(summed[0], home(0)), permuted(summed[1], home(1))
    shifted = permuted(activated[1], lambda x, q, z: device(NQ * x + q + 1, z))
    shifted, bias_rows = lax.optimization_barrier((shifted, bias_rows))
    activated = jnp.stack([shifted, activated[0]])
    grad_bias = bias_rows[0] + bias_rows[1]
    second, grad_filters = lax.optimization_barrier((second, grad_filters))
    grad_input = jnp.stack([second, first])
    shape = (2, GRID, GRID)
    return (
        activated.reshape(*shape, out_size),
        grad_input.reshape(*shape, size),
        grad_filters.transpose(1, 0, 2),
        grad_bias,
    )


def solution(mesh):
    return jax.shard_map(
        on_device,
        mesh=mesh,
        in_specs=(
            P("space", None, None, "chan"),
            P("space", None, "chan"),
            P("chan"),
            P("space", None, None, "chan"),
        ),
        out_specs=(
            P("space", None, None, "chan"),
            P("space", None, None, "chan"),
            P("space", None, "chan"),
            P("chan"),
        ),
        check_vma=False,
    )
```

```python
import math

import jax
import jax.numpy as jnp
from jax import lax
from jax.experimental import pallas as pl
from jax.experimental.pallas import tpu as pltpu
from jax.sharding import PartitionSpec as P


GRID = 16
FACE = GRID * GRID
NX, NQ, NZ = 4, 8, 8
KAPPA = 0.7978845608028654
CUBIC = 0.044715
VMEM_LIMIT = 24 * 1024 * 1024
Z_STEPS = (0, 4, 1, -3, -1, 3, 2, -2)


def gelu_pair(values):
    inner = KAPPA * (values + CUBIC * values * values * values)
    tangent = jnp.tanh(inner)
    output = 0.5 * values * (1.0 + tangent)
    slope = 0.5 * (1.0 + tangent) + 0.5 * values * (1.0 - tangent * tangent) * KAPPA * (
        1.0 + 3.0 * CUBIC * values * values
    )
    return (output, slope)


def device(space, z):
    return space % (NX * NQ) * NZ + z % NZ


def at(x, q, z):
    return device(x % NX * NQ + q % NQ, z)


def permuted(array, target):
    pairs = [(at(x, q, z), target(x, q, z)) for x in range(NX) for q in range(NQ) for z in range(NZ)]
    return lax.ppermute(array, ("space", "chan"), pairs)


def group(q):
    return q // 2 + 4 * (q % 2)


def holder(group):
    return group % 4 * 2 + group // 4


def swapped(index):
    return index >> 1 | (index & 1) << 1


def position(where):
    space, z = where[0], where[1]
    q = space & (NQ - 1)
    return space >> 3, q, q >> 1, q & 1, z


def ring_pairs(where, steps):
    _, _, y, core, z = position(where)
    return [(z + r - y - 4 * core) & (NQ - 1) for r in steps]


def slope_pairs(where):
    _, _, y, core, _ = position(where)
    rows = [(y - r) & 3 for r in range(4)]
    return [2 * row + core for row in rows] + [2 * row + 1 - core for row in rows]


def store_columns(pairs, planes, columns):
    size = planes[0].shape[-1]
    width = lax.broadcasted_iota(jnp.int32, (FACE, size), 0) % GRID
    rows, whole = columns.shape[1:]
    columns[0] = jnp.zeros((rows, whole), jnp.bfloat16)
    columns[GRID + 1] = jnp.zeros((rows, whole), jnp.bfloat16)
    edge = jnp.zeros((GRID, whole), jnp.bfloat16)
    places = [(ref, 2 * index) for ref in planes for index in range(ref.shape[0] // 2)]
    for pair, (ref, start) in zip(pairs, places):
        for half in range(2):
            depth = 2 * pair + half + 1
            middle = ref[start + half]
            wide = middle.astype(jnp.float32)
            left = jnp.where(width == 0, 0.0, pltpu.roll(wide, 1, 0)).astype(jnp.bfloat16)
            right = jnp.where(width == GRID - 1, 0.0, pltpu.roll(wide, FACE - 1, 0)).astype(
                jnp.bfloat16
            )
            columns[depth, :GRID, :] = edge
            columns[depth, FACE + GRID :, :] = edge
            for c, value in enumerate((left, middle, right)):
                columns[depth, GRID : FACE + GRID, c * size : (c + 1) * size] = value


def window(columns, plane):
    return jnp.concatenate(
        [columns[plane, GRID * b : GRID * b + FACE, :] for b in range(3)], axis=1
    )


def convolved(columns, pairs, paired):
    left = jnp.concatenate(
        [
            jnp.concatenate([window(columns, 2 * pair + i) for i in range(4)], axis=1)
            for pair in pairs
        ],
        axis=0,
    )
    return jnp.dot(left, paired[...], preferred_element_type=jnp.float32)


def halves(product, index, size):
    rows = slice(index * FACE, (index + 1) * FACE)
    return [product[rows, o * size : (o + 1) * size] for o in range(2)]


def weights_kernel(turned, where, *refs):
    *blocks, paired, natural = refs
    rows = blocks[0].shape[1]
    x = position(where)[0]
    for r in range(NX):
        offset = pl.multiple_of(swapped((x + r) & (NX - 1)) * rows, rows)
        for tap in range(27):
            natural[tap, pl.ds(offset, rows)] = blocks[r][tap]
    deep, wide = natural.shape[1:][::-1] if turned else natural.shape[1:]
    none = jnp.zeros((9 * deep, wide), jnp.bfloat16)
    paired[: 9 * deep, wide:] = none
    paired[27 * deep :, :wide] = none
    for tap in range(27):
        block = natural[tap]
        if turned:
            block = block.T
        a, bc = (26 - tap) // 9 if turned else tap // 9, (26 - tap) % 9 if turned else tap % 9
        for o in range(2):
            first = ((a + o) * 9 + bc) * deep
            paired[first : first + deep, o * wide : (o + 1) * wide] = block


def own_pairs(where):
    _, _, y, core, _ = position(where)
    return [2 * ((y + r) & 3) + core for r in range(4)]


def other_pairs(where):
    _, _, y, core, _ = position(where)
    return [2 * ((y + r) & 3) + 1 - core for r in range(4)]


def slopes_kernel(where, *refs):
    store_columns(slope_pairs(where), refs[:NQ], refs[NQ])


def product_kernel(pairs, where, columns, paired, *outs):
    product = convolved(columns, pairs(where), paired)
    places = [(out, 2 * index) for out in outs for index in range(out.shape[0] // 2)]
    for index, (out, start) in enumerate(places):
        for half, value in enumerate(halves(product, index, out.shape[-1])):
            out[start + half] = value.astype(out.dtype)


def filters_kernel(scale, where, columns, *refs):
    planes, outs = refs[:NQ], refs[NQ : NQ + NX]
    turned, total, natural = refs[NQ + NX :]
    size, rows = natural.shape[-1], outs[0].shape[1]
    x = position(where)[0]
    turned[:, :FACE] = jnp.zeros((size, FACE), jnp.bfloat16)
    turned[:, (GRID + 1) * FACE :] = jnp.zeros((size, FACE), jnp.bfloat16)
    bias = jnp.zeros((8, size), jnp.float32)
    for pair, ref in zip(slope_pairs(where), planes):
        for half in range(2):
            value = ref[half].astype(jnp.float32)
            bias = bias + jnp.sum(value.reshape(FACE // 8, 8, size), axis=0)
            start = pl.multiple_of((2 * pair + half + 1) * FACE, FACE)
            turned[:, pl.ds(start, FACE)] = ref[half].T
    product = None
    for first in range(0, GRID, GRID // 2):
        left = jnp.concatenate(
            [turned[:, (first + 2 - a) * FACE : (first + 2 - a + GRID // 2) * FACE] for a in range(3)],
            axis=0,
        )
        right = jnp.concatenate(
            [window(columns, first + 1 + e) for e in range(GRID // 2)], axis=0
        )
        part = jnp.dot(left, right, preferred_element_type=jnp.float32)
        product = part if product is None else product + part
    total[...] = product
    for tap in range(27):
        a, bc = tap // 9, tap % 9
        block = total[a * size : (a + 1) * size, bc * size : (bc + 1) * size]
        natural[tap] = (block * scale).astype(jnp.bfloat16).T
    whole = jnp.sum(bias, axis=0, keepdims=True) * scale
    upper = whole.astype(jnp.bfloat16)
    lower = (whole - upper.astype(jnp.float32)).astype(jnp.bfloat16)
    row = lax.broadcasted_iota(jnp.int32, (rows, size), 0)
    spread = jnp.where(
        row == 0, upper.astype(jnp.float32), jnp.where(row == 1, lower.astype(jnp.float32), 0.0)
    )
    for r in range(NX):
        offset = pl.multiple_of(swapped((x + r) & (NX - 1)) * rows, rows)
        for tap in range(27):
            outs[r][tap] = natural[tap, pl.ds(offset, rows)]
        outs[r][27] = spread.astype(outs[r].dtype)


def call(kernel, where, operands, outs, scratch, flops):
    moved = sum(o.size * o.dtype.itemsize for o in operands)
    moved += sum(math.prod(o.shape) * o.dtype.itemsize for o in outs)
    vmem = pl.BlockSpec(memory_space=pltpu.VMEM)
    return pl.pallas_call(
        kernel,
        out_shape=outs,
        in_specs=[pl.BlockSpec(memory_space=pltpu.SMEM)] + [vmem] * len(operands),
        out_specs=[vmem] * len(outs),
        scratch_shapes=scratch,
        compiler_params=pltpu.CompilerParams(vmem_limit_bytes=VMEM_LIMIT),
        cost_estimate=pl.CostEstimate(flops=flops, bytes_accessed=moved, transcendentals=0),
    )(where, *operands)


def on_device(features, filters, conv_bias, cotangent):
    where = jnp.stack([lax.axis_index("space"), lax.axis_index("chan")]).astype(jnp.int32)
    size, rows = features.shape[-1], filters.shape[0]
    out_size = filters.shape[-1]
    bf16, f32 = jnp.bfloat16, jnp.float32
    shaped = jax.ShapeDtypeStruct

    def along_z(piece, r):
        return permuted(piece, lambda x, q, z: at(x, q, z + r))

    block = permuted(
        filters.transpose(1, 0, 2),
        lambda x, q, z: at(swapped(q % NX), holder((NQ * x + q) // NX), z),
    )
    seconds = permuted(
        jnp.stack([features[0], cotangent[0]]), lambda x, q, z: device(NQ * x + q - 1, z)
    )
    ahead = seconds[1]
    own = jnp.stack([features[1], seconds[0]]).reshape(2, FACE, size)
    own = jnp.concatenate(
        [permuted(own, lambda x, q, z: at(x, holder(z), z + q + step)) for step in (0, 4)]
    )
    blocks = [block] * NX
    for shift in (2, 1, 3):
        blocks[shift] = permuted(block, lambda x, q, z: at(x - shift, q, z))
    above, below = along_z(own, -1), along_z(own, 1)
    above, below, block = lax.optimization_barrier((above, below, block))
    planes = [own, above, below, along_z(above[:2], -1), along_z(below[:2], 1)]

    flops = 2 * 27 * GRID * FACE * size * out_size
    paired_shape = lambda deep, wide: shaped((36 * deep, 2 * wide), bf16)
    columns_shape = shaped((GRID + 2, FACE + 2 * GRID, 3 * size), bf16)
    (columns,) = call(
        lambda where, *refs: store_columns(ring_pairs(where, Z_STEPS), refs[:-1], refs[-1]),
        where,
        planes,
        [columns_shape],
        [],
        0,
    )

    def weights(turned, where):
        (paired,) = call(
            lambda *refs: weights_kernel(turned, *refs),
            where,
            blocks,
            [paired_shape(out_size, size) if turned else paired_shape(size, out_size)],
            [pltpu.VMEM((27, size, out_size), bf16)],
            0,
        )
        return paired

    ahead_weights = weights(False, where)
    def products(pairs, where, columns, weights, outs):
        return call(
            lambda *refs: product_kernel(pairs, *refs),
            where,
            [columns, weights],
            outs,
            [],
            flops // 2,
        )

    (send,) = products(other_pairs, where, columns, ahead_weights, [shaped((8, FACE, out_size), bf16)])
    where, send = lax.optimization_barrier((where, send))
    send = permuted(send, lambda x, q, z: at(x, q ^ 1, z)).astype(f32)
    keep = products(own_pairs, where, columns, ahead_weights, [shaped((2, FACE, out_size), f32)] * 4)
    keep = [piece + send[2 * r : 2 * r + 2] for r, piece in enumerate(keep)]
    pre_act = keep[0]
    for r in (2, 1, 3):
        pre_act = pre_act + permuted(
            keep[r].astype(bf16), lambda x, q, z: at(x, q + 2 * r, z)
        ).astype(f32)
    back_weights = weights(True, where)
    pre_act, back_weights = lax.optimization_barrier((pre_act, back_weights))
    pre_act = pre_act + conv_bias[None, None, :]

    target = jnp.stack([cotangent[1], ahead])
    output, slope = gelu_pair(pre_act)
    activated = output.astype(bf16)
    grad_pre = (target.reshape(2, FACE, out_size).astype(f32) * slope).astype(bf16)

    slopes = [grad_pre]
    for r in range(1, 4):
        slopes.append(permuted(grad_pre, lambda x, q, z: at(x, q + 2 * r, z)))
    other = [permuted(piece, lambda x, q, z: at(x, q ^ 1, z)) for piece in slopes]
    slopes = slopes + other
    (slope_columns,) = call(slopes_kernel, where, slopes, [columns_shape], [], 0)

    scale = 1.0 / math.sqrt(NX * GRID * FACE)
    terms = call(
        lambda *refs: filters_kernel(scale, *refs),
        where,
        [columns] + slopes,
        [shaped((28, rows, out_size), bf16)] * NX,
        [
            pltpu.VMEM((out_size, (GRID + 2) * FACE), bf16),
            pltpu.VMEM((3 * out_size, 9 * size), f32),
            pltpu.VMEM((27, size, out_size), bf16),
        ],
        flops,
    )
    where, terms = lax.optimization_barrier((where, terms))
    def parts(steps, where, outs):
        return call(
            lambda *refs: product_kernel(lambda where: ring_pairs(where, steps), *refs),
            where,
            [slope_columns, back_weights],
            outs,
            [],
            flops * len(steps) // NZ,
        )

    received = [permuted(terms[2], lambda x, q, z: at(x + 2, q, z))]
    up, down = parts((2, -3, -2, 3), where, [shaped((4, FACE, size), bf16)] * 2)
    up, down, where = lax.optimization_barrier((up, down, where))
    up, down = along_z(up, 1), along_z(down, -1)
    above, below, beyond, summed = parts((1, -1, 4, 0), where, [shaped((2, FACE, size), f32)] * 4)
    above, below, beyond, summed, *later = lax.optimization_barrier(
        (above, below, beyond, summed, terms[1], terms[3])
    )
    received.append(permuted(later[0], lambda x, q, z: at(x + 1, q, z)))
    received.append(permuted(later[1], lambda x, q, z: at(x + 3, q, z)))
    above = (above + up[:2].astype(f32)).astype(bf16)
    below = (below + down[:2].astype(f32)).astype(bf16)
    beyond = (beyond + up[2:].astype(f32) + down[2:].astype(f32)).astype(bf16)
    beyond, above, below = along_z(beyond, 4), along_z(above, 1), along_z(below, -1)
    held = sum((piece.astype(f32) for piece in received), terms[0].astype(f32))
    grad_bias = held[27, 0] + held[27, 1]
    grad_filters = permuted(
        held[:27].astype(bf16), lambda x, q, z: device(NX * group(q) + swapped(x), z)
    ).astype(f32)
    summed = summed + beyond.astype(f32) + above.astype(f32) + below.astype(f32)
    summed, activated = lax.optimization_barrier((summed.astype(bf16), activated))

    def home(half):
        return lambda x, q, z: device(NQ * x + (z - group(q)) % NZ + half, group(q))

    first, second = permuted(summed[0], home(0)), permuted(summed[1], home(1))
    shifted = permuted(activated[1], lambda x, q, z: device(NQ * x + q + 1, z))
    activated = jnp.stack([shifted, activated[0]])
    second, grad_filters = lax.optimization_barrier((second, grad_filters))
    grad_input = jnp.stack([second, first])
    shape = (2, GRID, GRID)
    return (
        activated.reshape(*shape, out_size),
        grad_input.reshape(*shape, size),
        grad_filters.transpose(1, 0, 2),
        grad_bias,
    )


def solution(mesh):
    return jax.shard_map(
        on_device,
        mesh=mesh,
        in_specs=(
            P("space", None, None, "chan"),
            P("space", None, "chan"),
            P("chan"),
            P("space", None, None, "chan"),
        ),
        out_specs=(
            P("space", None, None, "chan"),
            P("space", None, None, "chan"),
            P("space", None, "chan"),
            P("chan"),
        ),
        check_vma=False,
    )
```

```python
import math

import jax
import jax.numpy as jnp
from jax import lax
from jax.experimental import pallas as pl
from jax.experimental.pallas import tpu as pltpu
from jax.sharding import PartitionSpec as P


GRID = 16
FACE = GRID * GRID
NX, NQ, NZ = 4, 8, 8
KAPPA = 0.7978845608028654
CUBIC = 0.044715
VMEM_LIMIT = 24 * 1024 * 1024
Z_STEPS = (0, 4, 1, -3, -1, 3, 2, -2)


def gelu_pair(values):
    inner = KAPPA * (values + CUBIC * values * values * values)
    tangent = jnp.tanh(inner)
    output = 0.5 * values * (1.0 + tangent)
    slope = 0.5 * (1.0 + tangent) + 0.5 * values * (1.0 - tangent * tangent) * KAPPA * (
        1.0 + 3.0 * CUBIC * values * values
    )
    return (output, slope)


def device(space, z):
    return space % (NX * NQ) * NZ + z % NZ


def at(x, q, z):
    return device(x % NX * NQ + q % NQ, z)


def permuted(array, target):
    pairs = [(at(x, q, z), target(x, q, z)) for x in range(NX) for q in range(NQ) for z in range(NZ)]
    return lax.ppermute(array, ("space", "chan"), pairs)


def group(q):
    return q // 2 + 4 * (q % 2)


def holder(group):
    return group % 4 * 2 + group // 4


def swapped(index):
    return index >> 1 | (index & 1) << 1


def position(where):
    space, z = where[0], where[1]
    q = space & (NQ - 1)
    return space >> 3, q, q >> 1, q & 1, z


def ring_pairs(where, steps):
    _, _, y, core, z = position(where)
    return [(z + r - y - 4 * core) & (NQ - 1) for r in steps]


def slope_pairs(where):
    _, _, y, core, _ = position(where)
    rows = [(y - r) & 3 for r in range(4)]
    return [2 * row + core for row in rows] + [2 * row + 1 - core for row in rows]


def store_columns(pairs, planes, columns):
    size = planes[0].shape[-1]
    width = lax.broadcasted_iota(jnp.int32, (FACE, size), 0) % GRID
    rows, whole = columns.shape[1:]
    columns[0] = jnp.zeros((rows, whole), jnp.bfloat16)
    columns[GRID + 1] = jnp.zeros((rows, whole), jnp.bfloat16)
    edge = jnp.zeros((GRID, whole), jnp.bfloat16)
    places = [(ref, 2 * index) for ref in planes for index in range(ref.shape[0] // 2)]
    for pair, (ref, start) in zip(pairs, places):
        for half in range(2):
            depth = 2 * pair + half + 1
            middle = ref[start + half]
            wide = middle.astype(jnp.float32)
            left = jnp.where(width == 0, 0.0, pltpu.roll(wide, 1, 0)).astype(jnp.bfloat16)
            right = jnp.where(width == GRID - 1, 0.0, pltpu.roll(wide, FACE - 1, 0)).astype(
                jnp.bfloat16
            )
            columns[depth, :GRID, :] = edge
            columns[depth, FACE + GRID :, :] = edge
            for c, value in enumerate((left, middle, right)):
                columns[depth, GRID : FACE + GRID, c * size : (c + 1) * size] = value


def window(columns, plane):
    return jnp.concatenate(
        [columns[plane, GRID * b : GRID * b + FACE, :] for b in range(3)], axis=1
    )


def convolved(columns, pairs, paired):
    left = jnp.concatenate(
        [
            jnp.concatenate([window(columns, 2 * pair + i) for i in range(4)], axis=1)
            for pair in pairs
        ],
        axis=0,
    )
    return jnp.dot(left, paired[...], preferred_element_type=jnp.float32)


def halves(product, index, size):
    rows = slice(index * FACE, (index + 1) * FACE)
    return [product[rows, o * size : (o + 1) * size] for o in range(2)]


def weights_kernel(turned, where, *refs):
    *blocks, paired, natural = refs
    rows = blocks[0].shape[1]
    x = position(where)[0]
    for r in range(NX):
        offset = pl.multiple_of(swapped((x + r) & (NX - 1)) * rows, rows)
        for tap in range(27):
            natural[tap, pl.ds(offset, rows)] = blocks[r][tap]
    deep, wide = natural.shape[1:][::-1] if turned else natural.shape[1:]
    none = jnp.zeros((9 * deep, wide), jnp.bfloat16)
    paired[: 9 * deep, wide:] = none
    paired[27 * deep :, :wide] = none
    for tap in range(27):
        block = natural[tap]
        if turned:
            block = block.T
        a, bc = (26 - tap) // 9 if turned else tap // 9, (26 - tap) % 9 if turned else tap % 9
        for o in range(2):
            first = ((a + o) * 9 + bc) * deep
            paired[first : first + deep, o * wide : (o + 1) * wide] = block


def own_pairs(where):
    _, _, y, core, _ = position(where)
    return [2 * ((y + r) & 3) + core for r in range(4)]


def other_pairs(where):
    _, _, y, core, _ = position(where)
    return [2 * ((y + r) & 3) + 1 - core for r in range(4)]


def slopes_kernel(where, *refs):
    store_columns(slope_pairs(where), refs[:NQ], refs[NQ])


def product_kernel(pairs, where, columns, paired, *outs):
    product = convolved(columns, pairs(where), paired)
    places = [(out, 2 * index) for out in outs for index in range(out.shape[0] // 2)]
    for index, (out, start) in enumerate(places):
        for half, value in enumerate(halves(product, index, out.shape[-1])):
            out[start + half] = value.astype(out.dtype)


def filters_kernel(scale, where, columns, *refs):
    planes, outs = refs[:NQ], refs[NQ : NQ + NX]
    turned, total, natural = refs[NQ + NX :]
    size, rows = natural.shape[-1], outs[0].shape[1]
    x = position(where)[0]
    turned[:, :FACE] = jnp.zeros((size, FACE), jnp.bfloat16)
    turned[:, (GRID + 1) * FACE :] = jnp.zeros((size, FACE), jnp.bfloat16)
    bias = jnp.zeros((8, size), jnp.float32)
    for pair, ref in zip(slope_pairs(where), planes):
        for half in range(2):
            value = ref[half].astype(jnp.float32)
            bias = bias + jnp.sum(value.reshape(FACE // 8, 8, size), axis=0)
            start = pl.multiple_of((2 * pair + half + 1) * FACE, FACE)
            turned[:, pl.ds(start, FACE)] = ref[half].T
    product = None
    for first in range(0, GRID, GRID // 2):
        left = jnp.concatenate(
            [turned[:, (first + 2 - a) * FACE : (first + 2 - a + GRID // 2) * FACE] for a in range(3)],
            axis=0,
        )
        right = jnp.concatenate(
            [window(columns, first + 1 + e) for e in range(GRID // 2)], axis=0
        )
        part = jnp.dot(left, right, preferred_element_type=jnp.float32)
        product = part if product is None else product + part
    total[...] = product
    for tap in range(27):
        a, bc = tap // 9, tap % 9
        block = total[a * size : (a + 1) * size, bc * size : (bc + 1) * size]
        natural[tap] = (block * scale).astype(jnp.bfloat16).T
    whole = jnp.sum(bias, axis=0, keepdims=True) * scale
    upper = whole.astype(jnp.bfloat16)
    lower = (whole - upper.astype(jnp.float32)).astype(jnp.bfloat16)
    row = lax.broadcasted_iota(jnp.int32, (rows, size), 0)
    spread = jnp.where(
        row == 0, upper.astype(jnp.float32), jnp.where(row == 1, lower.astype(jnp.float32), 0.0)
    )
    for r in range(NX):
        offset = pl.multiple_of(swapped((x + r) & (NX - 1)) * rows, rows)
        for tap in range(27):
            outs[r][tap] = natural[tap, pl.ds(offset, rows)]
        outs[r][27] = spread.astype(outs[r].dtype)


def call(kernel, where, operands, outs, scratch, flops):
    moved = sum(o.size * o.dtype.itemsize for o in operands)
    moved += sum(math.prod(o.shape) * o.dtype.itemsize for o in outs)
    vmem = pl.BlockSpec(memory_space=pltpu.VMEM)
    return pl.pallas_call(
        kernel,
        out_shape=outs,
        in_specs=[pl.BlockSpec(memory_space=pltpu.SMEM)] + [vmem] * len(operands),
        out_specs=[vmem] * len(outs),
        scratch_shapes=scratch,
        compiler_params=pltpu.CompilerParams(vmem_limit_bytes=VMEM_LIMIT),
        cost_estimate=pl.CostEstimate(flops=flops, bytes_accessed=moved, transcendentals=0),
    )(where, *operands)


def on_device(features, filters, conv_bias, cotangent):
    where = jnp.stack([lax.axis_index("space"), lax.axis_index("chan")]).astype(jnp.int32)
    size, rows = features.shape[-1], filters.shape[0]
    out_size = filters.shape[-1]
    bf16, f32 = jnp.bfloat16, jnp.float32
    shaped = jax.ShapeDtypeStruct

    def along_z(piece, r):
        return permuted(piece, lambda x, q, z: at(x, q, z + r))

    block = permuted(
        filters.transpose(1, 0, 2),
        lambda x, q, z: at(swapped(q % NX), holder((NQ * x + q) // NX), z),
    )
    seconds = permuted(
        jnp.stack([features[0], cotangent[0]]), lambda x, q, z: device(NQ * x + q - 1, z)
    )
    ahead = seconds[1]
    own = jnp.stack([features[1], seconds[0]]).reshape(2, FACE, size)
    own = jnp.concatenate(
        [permuted(own, lambda x, q, z: at(x, holder(z), z + q + step)) for step in (0, 4)]
    )
    blocks = [block] + [
        permuted(block, lambda x, q, z: at(x - shift, q, z)) for shift in range(1, NX)
    ]
    above, below = along_z(own, -1), along_z(own, 1)
    above, below, block = lax.optimization_barrier((above, below, block))
    planes = [own, above, below, along_z(above[:2], -1), along_z(below[:2], 1)]

    flops = 2 * 27 * GRID * FACE * size * out_size
    paired_shape = lambda deep, wide: shaped((36 * deep, 2 * wide), bf16)
    columns_shape = shaped((GRID + 2, FACE + 2 * GRID, 3 * size), bf16)
    (columns,) = call(
        lambda where, *refs: store_columns(ring_pairs(where, Z_STEPS), refs[:-1], refs[-1]),
        where,
        planes,
        [columns_shape],
        [],
        0,
    )
    columns, blocks[1], blocks[3] = lax.optimization_barrier((columns, blocks[1], blocks[3]))

    def weights(turned, where):
        (paired,) = call(
            lambda *refs: weights_kernel(turned, *refs),
            where,
            blocks,
            [paired_shape(out_size, size) if turned else paired_shape(size, out_size)],
            [pltpu.VMEM((27, size, out_size), bf16)],
            0,
        )
        return paired

    ahead_weights = weights(False, where)
    def products(pairs, where, columns, weights, outs):
        return call(
            lambda *refs: product_kernel(pairs, *refs),
            where,
            [columns, weights],
            outs,
            [],
            flops // 2,
        )

    (send,) = products(other_pairs, where, columns, ahead_weights, [shaped((8, FACE, out_size), bf16)])
    where, send = lax.optimization_barrier((where, send))
    send = permuted(send, lambda x, q, z: at(x, q ^ 1, z)).astype(f32)
    keep = products(own_pairs, where, columns, ahead_weights, [shaped((2, FACE, out_size), f32)] * 4)
    keep = [piece + send[2 * r : 2 * r + 2] for r, piece in enumerate(keep)]
    pre_act = keep[0]
    for r in (2, 1, 3):
        pre_act = pre_act + permuted(
            keep[r].astype(bf16), lambda x, q, z: at(x, q + 2 * r, z)
        ).astype(f32)
    back_weights = weights(True, where)
    pre_act, back_weights = lax.optimization_barrier((pre_act, back_weights))
    pre_act = pre_act + conv_bias[None, None, :]

    target = jnp.stack([cotangent[1], ahead])
    output, slope = gelu_pair(pre_act)
    activated = output.astype(bf16)
    grad_pre = (target.reshape(2, FACE, out_size).astype(f32) * slope).astype(bf16)

    slopes = [grad_pre]
    for r in range(1, 4):
        slopes.append(permuted(grad_pre, lambda x, q, z: at(x, q + 2 * r, z)))
    other = [permuted(piece, lambda x, q, z: at(x, q ^ 1, z)) for piece in slopes]
    slopes = slopes + other
    (slope_columns,) = call(slopes_kernel, where, slopes, [columns_shape], [], 0)

    scale = 1.0 / math.sqrt(NX * GRID * FACE)
    terms = call(
        lambda *refs: filters_kernel(scale, *refs),
        where,
        [columns] + slopes,
        [shaped((28, rows, out_size), bf16)] * NX,
        [
            pltpu.VMEM((out_size, (GRID + 2) * FACE), bf16),
            pltpu.VMEM((3 * out_size, 9 * size), f32),
            pltpu.VMEM((27, size, out_size), bf16),
        ],
        flops,
    )
    shifted = permuted(activated[1], lambda x, q, z: device(NQ * x + q + 1, z))
    where, terms, shifted = lax.optimization_barrier((where, terms, shifted))
    def parts(steps, where, outs):
        return call(
            lambda *refs: product_kernel(lambda where: ring_pairs(where, steps), *refs),
            where,
            [slope_columns, back_weights],
            outs,
            [],
            flops * len(steps) // NZ,
        )

    received = [permuted(terms[2], lambda x, q, z: at(x + 2, q, z))]
    up, down = parts((2, -3, -2, 3), where, [shaped((4, FACE, size), bf16)] * 2)
    up, down, where = lax.optimization_barrier((up, down, where))
    up, down = along_z(up, 1), along_z(down, -1)
    above, below, beyond, summed = parts((1, -1, 4, 0), where, [shaped((2, FACE, size), f32)] * 4)
    above, below, beyond, summed, *later = lax.optimization_barrier(
        (above, below, beyond, summed, terms[1], terms[3])
    )
    received.append(permuted(later[0], lambda x, q, z: at(x + 1, q, z)))
    received.append(permuted(later[1], lambda x, q, z: at(x + 3, q, z)))
    above = (above + up[:2].astype(f32)).astype(bf16)
    below = (below + down[:2].astype(f32)).astype(bf16)
    beyond = (beyond + up[2:].astype(f32) + down[2:].astype(f32)).astype(bf16)
    beyond, above, below = along_z(beyond, 4), along_z(above, 1), along_z(below, -1)
    held = sum((piece.astype(f32) for piece in received), terms[0].astype(f32))
    grad_bias = held[27, 0] + held[27, 1]
    grad_filters = permuted(
        held[:27].astype(bf16), lambda x, q, z: device(NX * group(q) + swapped(x), z)
    ).astype(f32)
    summed = summed + beyond.astype(f32) + above.astype(f32) + below.astype(f32)
    summed = summed.astype(bf16)

    def home(half):
        return lambda x, q, z: device(NQ * x + (z - group(q)) % NZ + half, group(q))

    first, second = permuted(summed[0], home(0)), permuted(summed[1], home(1))
    activated = jnp.stack([shifted, activated[0]])
    second, grad_filters = lax.optimization_barrier((second, grad_filters))
    grad_input = jnp.stack([second, first])
    shape = (2, GRID, GRID)
    return (
        activated.reshape(*shape, out_size),
        grad_input.reshape(*shape, size),
        grad_filters.transpose(1, 0, 2),
        grad_bias,
    )


def solution(mesh):
    return jax.shard_map(
        on_device,
        mesh=mesh,
        in_specs=(
            P("space", None, None, "chan"),
            P("space", None, "chan"),
            P("chan"),
            P("space", None, None, "chan"),
        ),
        out_specs=(
            P("space", None, None, "chan"),
            P("space", None, None, "chan"),
            P("space", None, "chan"),
            P("chan"),
        ),
        check_vma=False,
    )
```
